128 devices in a mesh: dp: 16 (over z, x), table: 8 (over y, core).
Axes of the slice: x: 4, y: 4, z: 4, core: 2. Of those that a mesh axis runs over, the one named last changes fastest.
Arguments:
- table: bfloat16 [524288, 512], P(('dp', 'table')), may hold values from -6 to 6
- w_in: bfloat16 [512, 2048], replicated, may hold values from -0.25 to 0.25
- w_out: bfloat16 [512, 512], replicated, may hold values from -0.25 to 0.25
- item_owner: int32 [3, 32768, 1], P(None, ('dp', 'table')), may hold values from 0 to 127; in each aligned block of 256 rows (0 to 255, 256 to 511, ..., all dimensions but the last counted through in order) at most 4 rows name the same one
- item_slot: int32 [3, 32768], P(None, ('dp', 'table')), may hold values from 0 to 4095
- seq_lengths: int32 [3, 128, 4], P(None, ('dp', 'table')), may hold values from 1 to 128, 256 in all within a row
- cotangent: bfloat16 [3, 32768, 512], P(None, ('dp', 'table')), may hold values from -6 to 6
Outputs:
- layer_out: bfloat16 [3, 32768, 512], P(None, ('dp', 'table'))
- table_grad: float32 [524288, 512], P(('dp', 'table'))
- w_in_grad: float32 [512, 2048], replicated
- w_out_grad: float32 [512, 512], replicated
The draws below stay inside these ranges and needn't reach their ends.
Inputs may be any that keep to these rules, and one draw needn't show every extreme that they name: `item_owner`: in every micro-batch, no owner is named by more than 4 of one device's 256 positions; some owner is named exactly 4 times. `seq_lengths`: each device's 4 lengths in a micro-batch sum to 256; the longest is 128.
All inputs are finite; a program needn't handle non-finite values.
Results may differ from the reference program's by a relative error of at most 0.019.
Values may be sent and summed in bfloat16 or wider, within the bound.
No kernel may reach another device: no remote copies, remote signals or barrier semaphores. Data moves between devices by JAX's collectives and lax.ppermute only.
A program may use at most 128 MiB of HBM per device.

```python
import math
import jax
import jax.numpy as jnp
import numpy as np
from jax import lax

D = 512
HEADS = 8
HEAD = 64
MB = 3
TOK_DEV = 256
SEQS = 4
MOST_LEN = 128
OWNERS = 128
TOKENS = 32768
ROWS_OWN = 4096
ITEMS = 524288
CAP = 4


def touch_ends(drawn, key, least, high):
    shape = drawn.shape
    index_at = [jax.random.randint(jax.random.fold_in(key, axis), (), 0, shape[axis]) for axis in range(len(shape))]
    drawn = drawn.at[tuple(index_at)].set(least)
    longest = shape.index(max(shape))
    index_at[longest] = (index_at[longest] + 1) % shape[longest]
    return drawn.at[tuple(index_at)].set(high)


def block_scale(own_key, extent, cuts, low, top_value):
    def one(position, shards_of):
        heights = jax.random.uniform(jax.random.fold_in(jax.random.fold_in(own_key, 6), position), (shards_of,), jnp.float32, low / len(cuts), top_value / len(cuts))
        return jnp.repeat(jnp.exp(heights), extent[position] // shards_of).reshape((-1,) + (1,) * (len(extent) - position - 1))

    factor_of = one(*cuts[0])
    for cut in cuts[1:]:
        factor_of = factor_of * one(*cut)
    return factor_of


def profile(count, total, bound, slope):
    weights = [(1 << 20) // math.isqrt(rank ** slope) + 1 for rank in range(2, count + 1)]
    surplus, counts = total - bound - (count - 1), [1] * (count - 1)
    while surplus > 0:
        candidates = [i for i in range(count - 1) if counts[i] < bound]
        pool, budget = sum([weights[i] for i in candidates]), surplus
        for i in candidates:
            addition = min(bound - counts[i], max(1, budget * weights[i] // pool), surplus)
            counts[i] = counts[i] + addition
            surplus = surplus - addition
    return np.array([bound] + counts)


def uneven(stream_key, count, total, bound, slope):
    if count == 2:
        one = jax.random.randint(stream_key, (), max(1, total - bound), min(bound, total - 1) + 1)
        return jnp.stack([one, total - one])
    sizes = jnp.asarray(profile(count, total, bound, slope), jnp.int32)
    pairs = (count - 1) // 2
    donor, taker = sizes[1:1 + 2 * pairs:2], sizes[2:2 + 2 * pairs:2]
    room = jnp.minimum(donor - 1, bound - taker)
    passed = jax.random.randint(jax.random.fold_in(stream_key, 1), (pairs,), 0, 1 << 20) % (room + 1)
    sizes = sizes.at[1:1 + 2 * pairs:2].set(donor - passed).at[2:2 + 2 * pairs:2].set(taker + passed)
    return sizes[jax.random.permutation(jax.random.fold_in(stream_key, 2), count)]


def deal_out(key, own, number, rows, amount, top, limit, skew):
    ranking = jax.random.permutation(key, amount)
    heavy_load, ordinary = shares(amount, rows * top, limit, skew, True), shares(amount, rows * top, limit, skew, False)
    places = jnp.arange(amount)

    def named(sizes, rotation):
        used = int((sizes > 0).sum())
        fixed = max(1, used // 4)
        shifted = fixed + (places - fixed + rotation * (used - fixed)) % max(1, amount - fixed)
        return jnp.zeros((amount,), jnp.int32).at[ranking[jnp.where(places < fixed, places, shifted)]].set(jnp.asarray(sizes, jnp.int32))

    sizes = jnp.where(number % 4 == 0, named(heavy_load, number // 4), named(ordinary, number - number // 4 - 1))
    mixed = jax.random.permutation(jax.random.fold_in(own, 3), amount)
    source_of, sink = mixed[0:amount // 2 * 2:2], mixed[1:amount // 2 * 2:2]
    margin = jnp.minimum(sizes[source_of] - 1, limit - sizes[sink]) // 2
    margin = jnp.where((source_of == ranking[0]) | (sink == ranking[0]) | (sizes[sink] == 0), 0, jnp.maximum(margin, 0))
    shifted = jax.random.randint(jax.random.fold_in(own, 4), (amount // 2,), 0, 1 << 20) % (margin + 1)
    sizes = sizes.at[source_of].add(-shifted).at[sink].add(shifted)
    labels = jnp.searchsorted(jnp.cumsum(sizes), jnp.arange(rows * top), side="right").astype(jnp.int32)
    table = labels.reshape(top, rows).T
    table = table[jax.random.permutation(jax.random.fold_in(own, 1), rows)]
    rotation = jax.random.randint(jax.random.fold_in(own, 2), (rows, 1), 0, top)
    return jnp.take_along_axis(table, (jnp.arange(top)[None, :] + rotation) % top, axis=1)


def shares(count, total, limit, slope, full):
    loads = [(1 << 20) // math.isqrt(rank ** slope) + 1 for rank in range(1, count + 1)]
    largest = limit if full else min(limit, max(-(-total // count), total * loads[0] // sum(loads)))
    least = 1 if total - largest >= count - 1 else 0
    given, rest = [largest] + [least] * (count - 1), total - largest - least * (count - 1)
    while rest > 0:
        candidates = [i for i in range(1, count) if given[i] < largest] or [i for i in range(1, count) if given[i] < limit]
        pool, budget = sum([loads[i] for i in candidates]), rest
        for i in candidates:
            extra = min(limit - given[i], max(1, budget * loads[i] // pool), rest)
            given[i] = given[i] + extra
            rest = rest - extra
    return np.array(given)


def bell_draw(stream_key, extent, width, bound, split=(), kind=jnp.bfloat16):
    gain = block_scale(stream_key, extent, split, -0.22, 0.18) if split else 1.0
    array = jax.random.normal(stream_key, extent, jnp.float32) * width * gain
    return jnp.minimum(jnp.maximum(array, -bound), bound).astype(kind)


def setup_inputs(seed: int = 0) -> dict:
    arg_keys = jax.random.split(jax.random.key(seed), 8)
    table = bell_draw(arg_keys[0], (ITEMS, D), 1.0, 6.0, ((0, 128),))
    w_in = bell_draw(arg_keys[1], (D, 4 * D), D ** -0.5, 0.25)
    w_out = bell_draw(arg_keys[2], (D, D), D ** -0.5, 0.25)
    item_owner_keys = jax.random.split(jax.random.fold_in(arg_keys[3], 1), MB * TOKENS // TOK_DEV)
    item_owner_turns = jax.random.permutation(jax.random.fold_in(arg_keys[3], 3), MB * TOKENS // TOK_DEV)
    item_owner = jax.vmap(lambda own, number: deal_out(jax.random.fold_in(arg_keys[3], 2), own, number, TOK_DEV, OWNERS, 1, CAP, 2))(item_owner_keys, item_owner_turns).reshape((MB, TOKENS, 1))
    item_slot = touch_ends(jax.random.randint(arg_keys[4], (MB, TOKENS), 0, ROWS_OWN), jax.random.fold_in(arg_keys[4], 1), 0, ROWS_OWN - 1).astype(jnp.int32)
    seq_lengths = jax.vmap(lambda own: uneven(own, SEQS, TOK_DEV, MOST_LEN, 2))(jax.random.split(arg_keys[5], MB * OWNERS)).reshape((MB, OWNERS, SEQS)).astype(jnp.int32)
    cotangent = bell_draw(arg_keys[6], (MB, TOKENS, D), 1.0, 6.0, ((1, 128),))
    return {"table": table, "w_in": w_in, "w_out": w_out, "item_owner": item_owner, "item_slot": item_slot, "seq_lengths": seq_lengths, "cotangent": cotangent}


def segment_ids(lengths):
    bounds = jnp.cumsum(lengths).astype(jnp.int32)
    places = jnp.arange(TOK_DEV, dtype=jnp.int32)
    return lax.optimization_barrier(jnp.sum((places[:, None] >= bounds[None, :]).astype(jnp.int32), axis=1))

def hstu_layer(embedded, w_in, w_out, segments):
    length = embedded.shape[0]
    hidden = jax.nn.silu(jnp.dot(embedded, w_in, preferred_element_type=jnp.float32)).astype(jnp.bfloat16)
    gate_part = hidden[:, :D]
    values = hidden[:, D:2 * D].reshape(length, HEADS, HEAD)
    queries = hidden[:, 2 * D:3 * D].reshape(length, HEADS, HEAD)
    keys = hidden[:, 3 * D:].reshape(length, HEADS, HEAD)
    scores = jnp.einsum('thd,shd->hts', queries.astype(jnp.float32), keys.astype(jnp.float32))
    places = jnp.arange(length, dtype=jnp.int32)
    allowed = (segments[:, None] == segments[None, :]) & (places[None, :] <= places[:, None])
    weights = jnp.where(allowed[None], jax.nn.silu(scores * HEAD ** (-0.5)), 0.0).astype(jnp.bfloat16)
    attended = jnp.einsum('hts,shd->thd', weights.astype(jnp.float32), values.astype(jnp.float32)).reshape(length, D)
    centred = attended - lax.optimization_barrier(jnp.mean(attended, axis=1, keepdims=True))
    normed = centred * lax.rsqrt(lax.optimization_barrier(jnp.mean(centred * centred, axis=1, keepdims=True)) + 1e-05)
    gated = (normed * gate_part.astype(jnp.float32)).astype(jnp.bfloat16)
    mixed = jnp.dot(gated, w_out, preferred_element_type=jnp.float32)
    return (embedded.astype(jnp.float32) + mixed).astype(jnp.bfloat16)

def reference(table, w_in, w_out, item_owner, item_slot, seq_lengths, cotangent):
    win_total = jnp.zeros((D, 4 * D), jnp.float32)
    wout_total = jnp.zeros((D, D), jnp.float32)
    outputs = []
    grads_all = []
    items_all = []
    for micro in range(MB):

        def one_device(carry, index):
            start = index * TOK_DEV
            owners = lax.dynamic_slice_in_dim(item_owner[micro, :, 0], start, TOK_DEV)
            slots = lax.dynamic_slice_in_dim(item_slot[micro], start, TOK_DEV)
            items = (owners * ROWS_OWN + slots).astype(jnp.int32)
            embedded = table[items]
            segments = segment_ids(seq_lengths[micro, index])
            target = lax.dynamic_slice_in_dim(cotangent[micro], start, TOK_DEV)

            def local_layer(emb_in, first, second):
                return hstu_layer(emb_in, first, second, segments)
            result, pullback = jax.vjp(local_layer, embedded, w_in, w_out)
            emb_grad, in_grad, out_grad = pullback(target)
            carry = (carry[0] + in_grad.astype(jnp.float32), carry[1] + out_grad.astype(jnp.float32))
            return (carry, (result, emb_grad, items))
        (win_total, wout_total), (result, emb_grad, items) = lax.scan(one_device, (win_total, wout_total), jnp.arange(OWNERS, dtype=jnp.int32))
        outputs.append(result.reshape(TOKENS, D))
        grads_all.append(emb_grad.reshape(TOKENS, D))
        items_all.append(items.reshape(TOKENS))
    layer_out = jnp.stack(outputs)
    every_item = jnp.concatenate(items_all).astype(jnp.int32)
    every_grad = jnp.concatenate(grads_all).astype(jnp.float32)
    table_grad = jnp.zeros((ITEMS, D), jnp.float32).at[every_item].add(every_grad)
    factor = (MB * TOKENS) ** (-0.5)
    return (layer_out, table_grad, win_total * factor, wout_total * factor)
```

```python
import functools

import jax
import jax.numpy as jnp
from jax import lax
from jax.experimental import pallas as pl
from jax.experimental.pallas import tpu as pltpu
from jax.sharding import PartitionSpec as P

HEADS = 8
MB = 3
CAP = 4
AXES = ("dp", "table")
F32 = jnp.float32
BF16 = jnp.bfloat16
I32 = jnp.int32
VMEM = pl.BlockSpec(memory_space=pltpu.VMEM)
SMEM = pl.BlockSpec(memory_space=pltpu.SMEM)


def iota(shape, dim):
    return lax.broadcasted_iota(I32, shape, dim)


def mm(a, b):
    return jnp.dot(a, b, preferred_element_type=F32)


def mm_nt(a, b):
    return lax.dot_general(a, b, (((1,), (1,)), ((), ())), preferred_element_type=F32)


def mm_tn(a, b):
    return lax.dot_general(a, b, (((0,), (0,)), ((), ())), preferred_element_type=F32)


def params(**more):
    return pltpu.CompilerParams(vmem_limit_bytes=48 * 1024 * 1024, **more)


def cost(flops, bytes_accessed):
    return pl.CostEstimate(flops=flops, bytes_accessed=bytes_accessed, transcendentals=0)


def request_kernel(owner_ref, slot_ref, wanted_ref, flat_ref):
    length = owner_ref.shape[1]
    owners_n = wanted_ref.shape[0]
    upto = (iota((length, length), 0) <= iota((length, length), 1)).astype(BF16)
    lane_row = iota((128, length), 0)
    high = jnp.zeros((owners_n, 128), F32)
    low = jnp.zeros((owners_n, 128), F32)
    live = jnp.zeros((owners_n, 128), F32)
    flat_ref[...] = jnp.zeros(flat_ref.shape, I32)
    for micro in range(MB):
        owner = owner_ref[micro : micro + 1, :]
        slot = slot_ref[micro : micro + 1, :]
        hot = (iota((owners_n, length), 0) == owner).astype(F32)
        hot_bf = hot.astype(BF16)
        counts = mm(hot_bf, upto)
        rank = (jnp.sum(counts * hot, axis=0, keepdims=True) - 1.0).astype(I32)
        flat_ref[micro : micro + 1, :] = owner * 8 + rank
        here = lane_row == rank + CAP * micro
        high = high + mm_nt(hot_bf, jnp.where(here, (slot >> 6).astype(F32), 0.0).astype(BF16))
        low = low + mm_nt(hot_bf, jnp.where(here, (slot & 63).astype(F32), 0.0).astype(BF16))
        live = live + mm_nt(hot_bf, jnp.where(here, 1.0, 0.0).astype(BF16))
    wanted_ref[...] = jnp.where(live > 0.5, high * 64.0 + low, -1.0).astype(I32)


def requests(owner, slot, owners_n):
    return pl.pallas_call(
        request_kernel,
        out_shape=(
            jax.ShapeDtypeStruct((owners_n, 128), I32),
            jax.ShapeDtypeStruct((8, owner.shape[1]), I32),
        ),
        in_specs=[VMEM, VMEM],
        out_specs=(VMEM, VMEM),
        compiler_params=params(),
        name="requests",
    )(owner, slot)


def gather_kernel(asked_ref, table_ref, out_ref, column_ref, sum_ref, *, first, width, steps):
    step = pl.program_id(0)
    rows = sum_ref.shape[0]
    block = table_ref.shape[0]

    @pl.when(step == 0)
    def _():
        asked = asked_ref[...]
        devices = asked.shape[0]
        spread = (iota((rows, devices), 0) // width == iota((rows, devices), 1)).astype(BF16)
        high = mm(spread, (asked >> 6).astype(F32).astype(BF16))
        low = mm(spread, (asked & 63).astype(F32).astype(BF16))
        mine = iota((rows, 128), 1) == iota((rows, 128), 0) % width + first
        column = jnp.sum(jnp.where(mine, high * 64.0 + low, 0.0), axis=1, keepdims=True)
        column_ref[...] = jnp.broadcast_to(column.astype(I32), column_ref.shape)

    column = column_ref[...][:, :1] - step * block
    hot = jnp.where(column == iota((rows, block), 1), 1.0, 0.0).astype(BF16)
    part = mm(hot, table_ref[...])

    @pl.when(step == 0)
    def _():
        sum_ref[...] = part

    @pl.when(step > 0)
    def _():
        sum_ref[...] += part

    @pl.when(step == steps - 1)
    def _():
        if width == 8:
            out_ref[...] = sum_ref[...].astype(BF16)
        else:
            whole = sum_ref[...].reshape(rows // 8, 8, sum_ref.shape[1])
            half = whole.shape[2] // 2
            left, right = whole[:, :, :half], whole[:, :, half:]
            top = iota(left.shape, 1) < 4
            even = jnp.where(top, left, pltpu.roll(right, 4, 1))
            odd = jnp.where(top, pltpu.roll(left, 4, 1), right)
            both = jnp.concatenate([even, odd], axis=1)
            out_ref[...] = both.reshape(out_ref.shape).astype(BF16)


def gather(asked, table, first, width):
    own_rows, columns = table.shape
    devices = asked.shape[0]
    steps = 4
    rows = devices * width
    out = (devices * 8, columns if width == 8 else columns // 2)
    return pl.pallas_call(
        functools.partial(gather_kernel, first=first, width=width, steps=steps),
        out_shape=jax.ShapeDtypeStruct(out, BF16),
        grid=(steps,),
        in_specs=[
            pl.BlockSpec((devices, 128), lambda i: (0, 0)),
            pl.BlockSpec((own_rows // steps, columns), lambda i: (i, 0)),
        ],
        out_specs=pl.BlockSpec(out, lambda i: (0, 0)),
        scratch_shapes=[pltpu.VMEM((rows, 128), I32), pltpu.VMEM((rows, columns), F32)],
        compiler_params=params(),
        cost_estimate=cost(2 * rows * own_rows * columns, 6 * 1024 * 1024),
        name=f"gather{width}",
    )(asked, table)


def column_of(row, copies=128):
    return jnp.transpose(jnp.broadcast_to(row.astype(F32), (copies, row.shape[1])))


def layer_kernel(
    lengths_ref,
    flat_ref,
    rows_ref,
    w_in_ref,
    w_out_ref,
    cot_ref,
    *rest,
    micro,
):
    out_ref, grad_ref, emb_t_ref, dpre_ref, gated_t_ref, hidden_ref, slope_ref, weight_ref, dsilu_ref, att_ref, datt_ref = (
        rest[-11:]
    )
    length, width = grad_ref.shape
    slots = rows_ref.shape[0]
    column = column_of(flat_ref[micro : micro + 1, :])

    def placing(shift):
        lanes = iota((length, 128), 1).astype(F32)
        parts = [
            jnp.where(column == lanes + float(first - shift), 1.0, 0.0).astype(BF16)
            for first in range(0, slots, 128)
        ]
        return jnp.concatenate(parts, axis=1)

    if micro == 0:
        rows = rows_ref[...]
        embedded = jnp.concatenate([mm(placing(0), rows), mm(placing(4), rows)], axis=1)
    else:
        embedded = mm(placing(4 * (micro - 1)), rows_ref[...])
    emb_t_ref[...] = jnp.transpose(embedded).astype(BF16)
    emb = embedded.astype(BF16)

    chunk = 512
    for first in range(0, 4 * width, chunk):
        at = slice(first, first + chunk)
        half = mm(emb, w_in_ref[:, at]) * 0.5
        tanh = jnp.tanh(half)
        act = half + half * tanh
        hidden_ref[:, at] = act.astype(BF16)
        slope_ref[:, at] = (0.5 * ((1.0 + tanh) + act * (1.0 - tanh))).astype(BF16)

    ends = []
    total = 0
    for which in range(3):
        total = total + lengths_ref[micro, 0, which]
        ends.append(total)

    def segment(places):
        return sum((places >= end).astype(I32) for end in ends)

    query_at = iota((length, length), 0)
    key_at = iota((length, length), 1)
    allowed = (segment(query_at) == segment(key_at)) & (key_at <= query_at)

    lane = iota((1, 128), 1)
    first_head = (lane < 64).astype(F32)
    second_head = 1.0 - first_head
    masks = (first_head.astype(BF16), second_head.astype(BF16))
    score_masks = ((first_head * 0.0625).astype(BF16), (second_head * 0.0625).astype(BF16))
    pairs = HEADS // 2
    for pair in range(pairs):
        lanes = slice(128 * pair, 128 * pair + 128)
        value = hidden_ref[:, width + 128 * pair : width + 128 * pair + 128]
        query = hidden_ref[:, 2 * width + 128 * pair : 2 * width + 128 * pair + 128]
        key = hidden_ref[:, 3 * width + 128 * pair : 3 * width + 128 * pair + 128]
        for head in range(2):
            half = mm_nt(query * score_masks[head], key)
            tanh = jnp.tanh(half)
            act = half + half * tanh
            at = slice(length * head, length * head + length)
            weight_ref[pair, :, at] = jnp.where(allowed, act, 0.0).astype(BF16)
            dsilu_ref[pair, :, at] = jnp.where(
                allowed, (1.0 + tanh) + act * (1.0 - tanh), 0.0
            ).astype(BF16)
        both = jnp.concatenate([value * masks[0], value * masks[1]], axis=0)
        att_ref[:, lanes] = mm(weight_ref[pair], both)

    attended = att_ref[...]
    centred = attended - jnp.mean(attended, axis=1, keepdims=True)
    inverse = lax.rsqrt(jnp.mean(centred * centred, axis=1, keepdims=True) + 1e-05)
    normed = centred * inverse
    gate = hidden_ref[:, :width].astype(F32)
    gated = normed * gate
    gated_t_ref[...] = jnp.transpose(gated).astype(BF16)
    cot = cot_ref[0]
    out_ref[0] = (embedded + mm(gated.astype(BF16), w_out_ref[...])).astype(BF16)

    dgated = mm_nt(cot, w_out_ref[...])
    dgate = dgated * normed
    dnormed = dgated * gate
    dpre_ref[:, :width] = (dgate * slope_ref[:, :width].astype(F32)).astype(BF16)
    shared = jnp.mean(dnormed * normed, axis=1, keepdims=True)
    dcentred = inverse * (dnormed - normed * shared)
    datt = dcentred - jnp.mean(dcentred, axis=1, keepdims=True)
    datt_ref[...] = datt.astype(BF16)

    for pair in range(pairs):
        at_value = slice(width + 128 * pair, width + 128 * pair + 128)
        at_query = slice(2 * width + 128 * pair, 2 * width + 128 * pair + 128)
        at_key = slice(3 * width + 128 * pair, 3 * width + 128 * pair + 128)
        value = hidden_ref[:, at_value]
        query = hidden_ref[:, at_query]
        key = hidden_ref[:, at_key]
        dhead = datt_ref[:, 128 * pair : 128 * pair + 128]
        parts = []
        for head in range(2):
            at = slice(length * head, length * head + length)
            dweight = mm_nt(dhead * masks[head], value)
            parts.append((dweight * dsilu_ref[pair, :, at].astype(F32)).astype(BF16))
        dscore = jnp.concatenate(parts, axis=1)
        both_keys = jnp.concatenate([key * score_masks[0], key * score_masks[1]], axis=0)
        dquery = mm(dscore, both_keys)
        dkeys = mm_tn(dscore, query * jnp.asarray(0.0625, BF16))
        dkey = jnp.where(lane < 64, dkeys[:length], dkeys[length:])
        dvalues = mm_tn(weight_ref[pair], dhead)
        dvalue = jnp.where(lane < 64, dvalues[:length], dvalues[length:])
        for at, grad in ((at_value, dvalue), (at_query, dquery), (at_key, dkey)):
            dpre_ref[:, at] = (grad * slope_ref[:, at].astype(F32)).astype(BF16)

    grad_ref[...] = (cot.astype(F32) + mm_nt(dpre_ref[...], w_in_ref[...])).astype(BF16)


def layer(lengths, flat, rows, w_in, w_out, cotangent, outputs, micro):
    width = w_in.shape[0]
    length = cotangent.shape[1]
    pairs = HEADS // 2
    block = pl.BlockSpec((1, length, width), lambda i: (micro, 0, 0))

    def whole(shape):
        return pl.BlockSpec(shape, lambda i: (0,) * len(shape))

    operands = [lengths, flat, rows, w_in, w_out, cotangent]
    in_specs = [SMEM, whole(flat.shape), whole(rows.shape), whole(w_in.shape), whole(w_out.shape), block]
    alias = {}
    if outputs is not None:
        alias = {len(operands): 0}
        operands.append(outputs)
        in_specs.append(pl.BlockSpec(memory_space=pl.ANY))
    return pl.pallas_call(
        functools.partial(layer_kernel, micro=micro),
        out_shape=(
            jax.ShapeDtypeStruct(cotangent.shape, BF16),
            jax.ShapeDtypeStruct((length, width), BF16),
            jax.ShapeDtypeStruct((width, length), BF16),
            jax.ShapeDtypeStruct((length, 4 * width), BF16),
            jax.ShapeDtypeStruct((width, length), BF16),
        ),
        grid=(1,),
        in_specs=in_specs,
        out_specs=(
            block,
            whole((length, width)),
            whole((width, length)),
            whole((length, 4 * width)),
            whole((width, length)),
        ),
        scratch_shapes=[
            pltpu.VMEM((length, 4 * width), BF16),
            pltpu.VMEM((length, 4 * width), BF16),
            pltpu.VMEM((pairs, length, 2 * length), BF16),
            pltpu.VMEM((pairs, length, 2 * length), BF16),
            pltpu.VMEM((length, width), F32),
            pltpu.VMEM((length, width), BF16),
        ],
        input_output_aliases=alias,
        compiler_params=params(),
        cost_estimate=cost(8_000_000_000, 6 * 1024 * 1024),
        name=f"layer{micro}",
    )(*operands)


def send_pair_kernel(flat_ref, first_ref, second_ref, out_ref):
    slots = out_ref.shape[0]
    length = first_ref.shape[0]
    places = iota((slots, length), 0)
    one = jnp.where(places == flat_ref[0:1, :], 1.0, 0.0).astype(BF16)
    two = jnp.where(places == flat_ref[1:2, :] + 4, 1.0, 0.0).astype(BF16)
    placing = jnp.concatenate([one, two], axis=1)
    grads = jnp.concatenate([first_ref[...], second_ref[...]], axis=0)
    out_ref[...] = mm(placing, grads).astype(BF16)


def send_pair(flat, first, second, slots):
    return pl.pallas_call(
        send_pair_kernel,
        out_shape=jax.ShapeDtypeStruct((slots, first.shape[1]), BF16),
        in_specs=[VMEM] * 3,
        out_specs=VMEM,
        compiler_params=params(),
        cost_estimate=cost(1_000_000_000, 2 * 1024 * 1024),
        name="send_pair",
    )(flat, first, second)


def weights_kernel(core_ref, *refs):
    embs, dpres, gateds, cots, out_ref = refs[0:3], refs[3:6], refs[6:9], refs[9], refs[10]
    width4 = dpres[0].shape[1]
    left = jnp.concatenate([ref[...] for ref in embs], axis=1)
    groups, _, columns = out_ref.shape[1:]
    right_out = jnp.concatenate([cots[m] for m in range(MB)], axis=0)
    left_out = jnp.concatenate([ref[...] for ref in gateds], axis=1)
    tail = mm(left_out, right_out).astype(BF16)
    for group in range(groups):
        first = group * columns
        last = min(first + columns, width4)
        right = jnp.concatenate([ref[:, first:last] for ref in dpres], axis=0)
        out_ref[0, group, :, : last - first] = mm(left, right).astype(BF16)
    kept = width4 - (groups - 1) * columns
    out_ref[0, groups - 1, :, kept:] = tail


def weight_grads(core, embs, dpres, gateds, cotangent):
    width, length = embs[0].shape
    width4 = dpres[0].shape[1]
    half = width // 2
    columns = (width4 + width) // 4
    split = pl.BlockSpec((half, length), lambda i, core: ((core[0] + i) % 2, 0))

    def whole(shape):
        return pl.BlockSpec(shape, lambda i, core: (0,) * len(shape))

    return pl.pallas_call(
        weights_kernel,
        out_shape=jax.ShapeDtypeStruct((2, 4, half, columns), BF16),
        grid_spec=pltpu.PrefetchScalarGridSpec(
            num_scalar_prefetch=1,
            grid=(2,),
            in_specs=[split] * 3 + [whole((length, width4))] * 3 + [split] * 3 + [whole(cotangent.shape)],
            out_specs=pl.BlockSpec((1, 4, half, columns), lambda i, core: (i, 0, 0, 0)),
        ),
        compiler_params=params(),
        cost_estimate=cost(2 * 768 * 512 * 2560, 8 * 1024 * 1024),
        name="weight_grads",
    )(core, *embs, *dpres, *gateds, cotangent)


def message_kernel(flat_ref, grad_ref, mine_ref, other_ref, out_ref):
    slots = out_ref.shape[0]
    length, width = grad_ref.shape
    half = width // 2
    places = iota((slots, length), 0)
    one = jnp.where(places == flat_ref[2:3, :], 1.0, 0.0).astype(BF16)
    two = jnp.where(places == flat_ref[2:3, :] + 4, 1.0, 0.0).astype(BF16)
    placing = jnp.concatenate([one, two], axis=1)
    grads = jnp.concatenate([grad_ref[:, :half], grad_ref[:, half:]], axis=0)
    out_ref[:, :half] = mm(placing, grads).astype(BF16)
    out_ref[:, half:] = (mine_ref[0].astype(F32) + other_ref[...].astype(F32)).astype(BF16)


def message(flat, grad, mine, other):
    slots, columns = other.shape
    width = grad.shape[1] // 2 + columns
    return pl.pallas_call(
        message_kernel,
        out_shape=jax.ShapeDtypeStruct((slots, width), BF16),
        grid=(1,),
        in_specs=[
            pl.BlockSpec(flat.shape, lambda i: (0, 0)),
            pl.BlockSpec(grad.shape, lambda i: (0, 0)),
            pl.BlockSpec((1, slots, columns), lambda i: (0, 0, 0)),
            pl.BlockSpec((slots, columns), lambda i: (0, 0)),
        ],
        out_specs=pl.BlockSpec((slots, width), lambda i: (0, 0)),
        compiler_params=params(),
        cost_estimate=cost(500_000_000, 6 * 1024 * 1024),
        name="message",
    )(flat, grad, mine, other)


def shard_sum_kernel(in_ref, out_ref, *, skip, factor):
    slots = in_ref.shape[0]
    parts = in_ref[:, skip:].astype(F32).reshape(slots // 16, 16, in_ref.shape[1] - skip)
    summed = (jnp.sum(parts, axis=0) * factor).astype(BF16)
    out_ref[...] = jnp.broadcast_to(summed[None], (slots // 16, *summed.shape)).reshape(out_ref.shape)


def shard_sum(arrived, skip, factor):
    slots = arrived.shape[0]
    return pl.pallas_call(
        functools.partial(shard_sum_kernel, skip=skip, factor=factor),
        out_shape=jax.ShapeDtypeStruct((slots, arrived.shape[1] - skip), BF16),
        in_specs=[VMEM],
        out_specs=VMEM,
        compiler_params=params(),
        cost_estimate=cost(1_000_000, 4 * 1024 * 1024),
        name="shard_sum",
    )(arrived)


def table_grad_kernel(pair_row_ref, last_row_ref, pair_ref, last_ref, out_ref, last_rows_ref, *, fold):
    step = pl.program_id(0)
    block = out_ref.shape[0]

    @pl.when(step == 0)
    def _():
        slots = last_ref.shape[0]
        folded = last_ref[:, :fold].astype(F32).reshape(slots // 16, 16, fold)
        even, odd = folded[:, :8], folded[:, 8:]
        top = iota(even.shape, 1) < 4
        left = jnp.where(top, even, pltpu.roll(odd, 4, 1))
        right = jnp.where(top, pltpu.roll(even, 4, 1), odd)
        last_rows_ref[...] = jnp.concatenate([left, right], axis=2).reshape(last_rows_ref.shape).astype(BF16)

    def hot(row):
        places = iota((block, row.shape[1]), 0)
        return jnp.where(places == row - step * block, 1.0, 0.0).astype(BF16)

    out_ref[...] = mm(hot(pair_row_ref[...]), pair_ref[...]) + mm(hot(last_row_ref[...]), last_rows_ref[...])


def table_gradient(pair_row, last_row, pair, last, own_rows):
    width = pair.shape[1]
    steps = 8
    block = own_rows // steps

    def whole(shape):
        return pl.BlockSpec(shape, lambda i: (0,) * len(shape))

    return pl.pallas_call(
        functools.partial(table_grad_kernel, fold=width // 2),
        out_shape=jax.ShapeDtypeStruct((own_rows, width), F32),
        grid=(steps,),
        in_specs=[whole(pair_row.shape), whole(last_row.shape), whole(pair.shape), whole(last.shape)],
        out_specs=pl.BlockSpec((block, width), lambda i: (i, 0)),
        scratch_shapes=[pltpu.VMEM((last_row.shape[1], width), BF16)],
        compiler_params=params(),
        cost_estimate=cost(2 * own_rows * 1536 * width, 12 * 1024 * 1024),
        name="table_grad",
    )(pair_row, last_row, pair, last)


def finish_kernel(core_ref, mine_ref, other_ref, win_ref, wout_ref):
    own = core_ref[0] == pl.program_id(0)
    groups, _, columns = mine_ref.shape
    width4 = win_ref.shape[1]

    def put(ref):
        for group in range(groups):
            first = group * columns
            last = min(first + columns, width4)
            win_ref[:, first:last] = ref[group, :, : last - first].astype(F32)
        wout_ref[...] = ref[groups - 1, :, width4 - (groups - 1) * columns :].astype(F32)

    @pl.when(own)
    def _():
        put(mine_ref)

    @pl.when(jnp.logical_not(own))
    def _():
        put(other_ref)


def finish(core, mine, other, width, width4):
    half = width // 2
    shape = mine.shape
    return pl.pallas_call(
        finish_kernel,
        out_shape=(jax.ShapeDtypeStruct((width, width4), F32), jax.ShapeDtypeStruct((width, width), F32)),
        grid_spec=pltpu.PrefetchScalarGridSpec(
            num_scalar_prefetch=1,
            grid=(2,),
            in_specs=[pl.BlockSpec(shape, lambda i, core: (0, 0, 0))] * 2,
            out_specs=(
                pl.BlockSpec((half, width4), lambda i, core: (i, 0)),
                pl.BlockSpec((half, width), lambda i, core: (i, 0)),
            ),
        ),
        compiler_params=params(),
        cost_estimate=cost(1_000_000, 8 * 1024 * 1024),
        name="finish",
    )(core, mine, other)


def trade(payload):
    return lax.all_to_all(payload, AXES, split_axis=0, concat_axis=0, tiled=True)


def shards(table, w_in, w_out, item_owner, item_slot, seq_lengths, cotangent):
    table_axis = lax.axis_size("table")
    owners_n = lax.axis_size("dp") * table_axis
    length = item_slot.shape[1]
    own_rows, width = table.shape
    slots = owners_n * 8
    core = (lax.axis_index("table") % 2).astype(I32).reshape(1)
    swap = [(i, i ^ 1) for i in range(table_axis)]

    wanted, flat = requests(item_owner.reshape(MB, length), item_slot, owners_n)
    asked = trade(wanted)
    rows_first = trade(gather(asked, table, 0, 4))
    rows_later = trade(gather(asked, table, 4, 8))
    pair_row = asked[:, :8].reshape(1, slots)
    last_row = asked[:, 8:12].reshape(1, slots // 2)

    out, grad0, emb0, dpre0, gated0 = layer(seq_lengths, flat, rows_first, w_in, w_out, cotangent, None, 0)
    out, grad1, emb1, dpre1, gated1 = layer(seq_lengths, flat, rows_later, w_in, w_out, cotangent, out, 1)
    incoming_pair = trade(send_pair(flat, grad0, grad1, slots))
    out, grad2, emb2, dpre2, gated2 = layer(seq_lengths, flat, rows_later, w_in, w_out, cotangent, out, 2)

    halves = weight_grads(core, (emb0, emb1, emb2), (dpre0, dpre1, dpre2), (gated0, gated1, gated2), cotangent)
    columns = halves.shape[3]
    halves = halves.reshape(2, slots, columns)
    other = lax.ppermute(halves[1], "table", swap)
    arrived = trade(message(flat, grad2, halves, other))
    factor = (MB * length * owners_n) ** (-0.5)
    mine_full = trade(shard_sum(arrived, width // 2, factor))
    other_full = lax.ppermute(mine_full, "table", swap)
    table_grad = table_gradient(pair_row, last_row, incoming_pair, arrived, own_rows)
    shape = (4, width // 2, columns)
    win_grad, wout_grad = finish(core, mine_full.reshape(shape), other_full.reshape(shape), width, w_in.shape[1])
    return out, table_grad, win_grad, wout_grad


def solution(mesh):
    in_specs = (
        P(AXES, None),
        P(),
        P(),
        P(None, AXES, None),
        P(None, AXES),
        P(None, AXES, None),
        P(None, AXES, None),
    )
    out_specs = (P(None, AXES, None), P(AXES, None), P(), P())
    return jax.shard_map(shards, mesh=mesh, in_specs=in_specs, out_specs=out_specs, check_vma=False)
```

```python
import functools

import jax
import jax.numpy as jnp
from jax import lax
from jax.experimental import pallas as pl
from jax.experimental.pallas import tpu as pltpu
from jax.sharding import PartitionSpec as P

HEADS = 8
MB = 3
CAP = 4
AXES = ("dp", "table")
F32 = jnp.float32
BF16 = jnp.bfloat16
I32 = jnp.int32
VMEM = pl.BlockSpec(memory_space=pltpu.VMEM)
HBM = pl.BlockSpec(memory_space=pltpu.HBM)
SMEM = pl.BlockSpec(memory_space=pltpu.SMEM)


def iota(shape, dim):
    return lax.broadcasted_iota(I32, shape, dim)


def mm(a, b):
    return jnp.dot(a, b, preferred_element_type=F32)


def mm_nt(a, b):
    return lax.dot_general(a, b, (((1,), (1,)), ((), ())), preferred_element_type=F32)


def mm_tn(a, b):
    return lax.dot_general(a, b, (((0,), (0,)), ((), ())), preferred_element_type=F32)


def params(mib):
    return pltpu.CompilerParams(vmem_limit_bytes=mib * 1024 * 1024)


def cost(flops, bytes_accessed):
    return pl.CostEstimate(flops=flops, bytes_accessed=bytes_accessed, transcendentals=0)


def request_kernel(owner_ref, slot_ref, wanted_ref, flat_ref):
    length = slot_ref.shape[1]
    owners_n = wanted_ref.shape[0]
    upto = (iota((length, length), 0) <= iota((length, length), 1)).astype(BF16)
    lane_row = iota((128, length), 0)
    high = jnp.zeros((owners_n, 128), F32)
    low = jnp.zeros((owners_n, 128), F32)
    live = jnp.zeros((owners_n, 128), F32)
    flat_ref[...] = jnp.zeros(flat_ref.shape, I32)
    for micro in range(MB):
        owner = owner_ref[micro]
        slot = slot_ref[micro : micro + 1, :]
        hot = (iota((owners_n, length), 0) == owner).astype(F32)
        hot_bf = hot.astype(BF16)
        counts = mm(hot_bf, upto)
        rank = (jnp.sum(counts * hot, axis=0, keepdims=True) - 1.0).astype(I32)
        flat_ref[micro : micro + 1, :] = owner * 8 + rank
        here = lane_row == rank + CAP * micro
        high = high + mm_nt(hot_bf, jnp.where(here, (slot >> 6).astype(F32), 0.0).astype(BF16))
        low = low + mm_nt(hot_bf, jnp.where(here, (slot & 63).astype(F32), 0.0).astype(BF16))
        live = live + mm_nt(hot_bf, jnp.where(here, 1.0, 0.0).astype(BF16))
    wanted_ref[...] = jnp.where(live > 0.5, high * 64.0 + low, -1.0).astype(I32)


def requests(owner, slot, owners_n):
    return pl.pallas_call(
        request_kernel,
        out_shape=(
            jax.ShapeDtypeStruct((owners_n, 128), I32),
            jax.ShapeDtypeStruct((8, slot.shape[1]), I32),
        ),
        grid=(1,),
        in_specs=[
            pl.BlockSpec(owner.shape, lambda i: (0, 0, 0)),
            pl.BlockSpec(slot.shape, lambda i: (0, 0)),
        ],
        out_specs=(
            pl.BlockSpec((owners_n, 128), lambda i: (0, 0)),
            pl.BlockSpec((8, slot.shape[1]), lambda i: (0, 0)),
        ),
        compiler_params=params(8),
        name="requests",
    )(owner, slot)


def gather_kernel(asked_ref, table_ref, out_ref, block_ref, sem, *, first, width, steps):
    devices = asked_ref.shape[0]
    rows = devices * width
    block = table_ref.shape[0] // steps
    copies = [
        pltpu.make_async_copy(table_ref.at[pl.ds(step * block, block)], block_ref.at[step], sem.at[step])
        for step in range(steps)
    ]
    for copy in copies:
        copy.start()
    asked = asked_ref[...]
    spread = (iota((rows, devices), 0) // width == iota((rows, devices), 1)).astype(BF16)
    high = mm(spread, (asked >> 6).astype(F32).astype(BF16))
    low = mm(spread, (asked & 63).astype(F32).astype(BF16))
    mine = iota((rows, 128), 1) == iota((rows, 128), 0) % width + first
    column = jnp.sum(jnp.where(mine, high * 64.0 + low, 0.0), axis=1, keepdims=True).astype(I32)
    found = None
    for step in range(steps):
        copies[step].wait()
        hot = jnp.where(column - step * block == iota((rows, block), 1), 1.0, 0.0).astype(BF16)
        part = mm(hot, block_ref[step])
        found = part if found is None else found + part
    if width == 8:
        out_ref[...] = found.astype(BF16)
    else:
        whole = found.reshape(rows // 8, 8, found.shape[1])
        half = whole.shape[2] // 2
        left, right = whole[:, :, :half], whole[:, :, half:]
        top = iota(left.shape, 1) < 4
        even = jnp.where(top, left, pltpu.roll(right, 4, 1))
        odd = jnp.where(top, pltpu.roll(left, 4, 1), right)
        both = jnp.concatenate([even, odd], axis=1)
        out_ref[...] = both.reshape(out_ref.shape).astype(BF16)


def gather(asked, table, first, width):
    own_rows, columns = table.shape
    devices = asked.shape[0]
    steps = 8
    rows = devices * width
    out = (devices * 8, columns if width == 8 else columns // 2)
    return pl.pallas_call(
        functools.partial(gather_kernel, first=first, width=width, steps=steps),
        out_shape=jax.ShapeDtypeStruct(out, BF16),
        grid=(1,),
        in_specs=[
            pl.BlockSpec((devices, 128), lambda i: (0, 0)),
            pl.BlockSpec(memory_space=pltpu.HBM),
        ],
        out_specs=pl.BlockSpec(out, lambda i: (0, 0)),
        scratch_shapes=[
            pltpu.VMEM((steps, own_rows // steps, columns), BF16),
            pltpu.SemaphoreType.DMA((steps,)),
        ],
        compiler_params=params(60),
        cost_estimate=cost(2 * rows * own_rows * columns, 6 * 1024 * 1024),
        name=f"gather{width}",
    )(asked, table)


def column_of(row, copies=128):
    return jnp.transpose(jnp.broadcast_to(row.astype(F32), (copies, row.shape[1])))


def layer_kernel(lengths_ref, flat_ref, rows_hbm, w_in_hbm, w_out_hbm, cot_hbm, *rest, micro):
    out_hbm, grad_hbm, emb_t_hbm, dpre_hbm, gated_t_hbm = rest[-23:-18]
    (
        rows_ref,
        w_in_ref,
        w_out_ref,
        cot_ref,
        out_ref,
        grad_ref,
        emb_t_ref,
        dpre_ref,
        gated_t_ref,
        hidden_ref,
        slope_ref,
        weight_ref,
        dsilu_ref,
        att_ref,
        datt_ref,
        in_sem,
        w_sem,
        out_sem,
    ) = rest[-18:]
    length, width = grad_ref.shape
    slots = rows_ref.shape[0]
    chunk = 512

    rows_copy = pltpu.make_async_copy(rows_hbm, rows_ref, in_sem.at[0])
    rows_copy.start()
    w_copies = []
    for which, first in enumerate(range(0, 4 * width, chunk)):
        at = pl.ds(first, chunk)
        w_copies.append(pltpu.make_async_copy(w_in_hbm.at[:, at], w_in_ref.at[:, at], w_sem.at[which]))
        w_copies[-1].start()
    w_out_copy = pltpu.make_async_copy(w_out_hbm, w_out_ref, in_sem.at[1])
    w_out_copy.start()
    cot_copy = pltpu.make_async_copy(cot_hbm.at[micro], cot_ref, in_sem.at[2])
    cot_copy.start()
    column = column_of(flat_ref[micro : micro + 1, :])

    def placing(shift):
        lanes = iota((length, 128), 1).astype(F32)
        parts = [
            jnp.where(column == lanes + float(first - shift), 1.0, 0.0).astype(BF16)
            for first in range(0, slots, 128)
        ]
        return jnp.concatenate(parts, axis=1)

    if micro == 2:
        places = (placing(0), placing(4))
        rows_copy.wait()
        rows = rows_ref[...]
        embedded = jnp.concatenate([mm(places[0], rows), mm(places[1], rows)], axis=1)
    else:
        places = placing(4 * micro)
        rows_copy.wait()
        embedded = mm(places, rows_ref[...])
    emb_t_ref[...] = jnp.transpose(embedded).astype(BF16)
    outgoing = [pltpu.make_async_copy(emb_t_ref, emb_t_hbm, out_sem.at[0])]
    outgoing[-1].start()
    emb = embedded.astype(BF16)

    for which, first in enumerate(range(0, 4 * width, chunk)):
        w_copies[which].wait()
        at = slice(first, first + chunk)
        half = mm(emb, w_in_ref[:, at]) * 0.5
        tanh = jnp.tanh(half)
        act = half + half * tanh
        hidden_ref[:, at] = act.astype(BF16)
        slope_ref[:, at] = (0.5 * ((1.0 + tanh) + act * (1.0 - tanh))).astype(BF16)

    ends = []
    total = 0
    for which in range(3):
        total = total + lengths_ref[micro, 0, which]
        ends.append(total)

    def segment(places):
        return sum((places >= end).astype(I32) for end in ends)

    query_at = iota((length, length), 0)
    key_at = iota((length, length), 1)
    allowed = (segment(query_at) == segment(key_at)) & (key_at <= query_at)

    lane = iota((1, 128), 1)
    first_head = (lane < 64).astype(F32)
    second_head = 1.0 - first_head
    masks = (first_head.astype(BF16), second_head.astype(BF16))
    score_masks = ((first_head * 0.0625).astype(BF16), (second_head * 0.0625).astype(BF16))
    pairs = HEADS // 2
    for pair in range(pairs):
        lanes = slice(128 * pair, 128 * pair + 128)
        value = hidden_ref[:, width + 128 * pair : width + 128 * pair + 128]
        query = hidden_ref[:, 2 * width + 128 * pair : 2 * width + 128 * pair + 128]
        key = hidden_ref[:, 3 * width + 128 * pair : 3 * width + 128 * pair + 128]
        for head in range(2):
            half = mm_nt(query * score_masks[head], key)
            tanh = jnp.tanh(half)
            act = half + half * tanh
            at = slice(length * head, length * head + length)
            weight_ref[pair, :, at] = jnp.where(allowed, act, 0.0).astype(BF16)
            dsilu_ref[pair, :, at] = jnp.where(
                allowed, (1.0 + tanh) + act * (1.0 - tanh), 0.0
            ).astype(BF16)
        both = jnp.concatenate([value * masks[0], value * masks[1]], axis=0)
        att_ref[:, lanes] = mm(weight_ref[pair], both)

    attended = att_ref[...]
    centred = attended - jnp.mean(attended, axis=1, keepdims=True)
    inverse = lax.rsqrt(jnp.mean(centred * centred, axis=1, keepdims=True) + 1e-05)
    normed = centred * inverse
    gate = hidden_ref[:, :width].astype(F32)
    gated = normed * gate
    gated_t_ref[...] = jnp.transpose(gated).astype(BF16)
    outgoing.append(pltpu.make_async_copy(gated_t_ref, gated_t_hbm, out_sem.at[1]))
    outgoing[-1].start()
    w_out_copy.wait()
    cot_copy.wait()
    cot = cot_ref[...]
    out_ref[...] = (embedded + mm(gated.astype(BF16), w_out_ref[...])).astype(BF16)
    outgoing.append(pltpu.make_async_copy(out_ref, out_hbm.at[micro], out_sem.at[2]))
    outgoing[-1].start()

    dgated = mm_nt(cot, w_out_ref[...])
    dgate = dgated * normed
    dnormed = dgated * gate
    dpre_ref[:, :width] = (dgate * slope_ref[:, :width].astype(F32)).astype(BF16)
    shared = jnp.mean(dnormed * normed, axis=1, keepdims=True)
    dcentred = inverse * (dnormed - normed * shared)
    datt = dcentred - jnp.mean(dcentred, axis=1, keepdims=True)
    datt_ref[...] = datt.astype(BF16)

    for pair in range(pairs):
        at_value = slice(width + 128 * pair, width + 128 * pair + 128)
        at_query = slice(2 * width + 128 * pair, 2 * width + 128 * pair + 128)
        at_key = slice(3 * width + 128 * pair, 3 * width + 128 * pair + 128)
        value = hidden_ref[:, at_value]
        query = hidden_ref[:, at_query]
        key = hidden_ref[:, at_key]
        dhead = datt_ref[:, 128 * pair : 128 * pair + 128]
        parts = []
        for head in range(2):
            at = slice(length * head, length * head + length)
            dweight = mm_nt(dhead * masks[head], value)
            parts.append((dweight * dsilu_ref[pair, :, at].astype(F32)).astype(BF16))
        dscore = jnp.concatenate(parts, axis=1)
        both_keys = jnp.concatenate([key * score_masks[0], key * score_masks[1]], axis=0)
        dquery = mm(dscore, both_keys)
        dkeys = mm_tn(dscore, query * jnp.asarray(0.0625, BF16))
        dkey = jnp.where(lane < 64, dkeys[:length], dkeys[length:])
        dvalues = mm_tn(weight_ref[pair], dhead)
        dvalue = jnp.where(lane < 64, dvalues[:length], dvalues[length:])
        for at, grad in ((at_value, dvalue), (at_query, dquery), (at_key, dkey)):
            dpre_ref[:, at] = (grad * slope_ref[:, at].astype(F32)).astype(BF16)

    outgoing.append(pltpu.make_async_copy(dpre_ref, dpre_hbm, out_sem.at[3]))
    outgoing[-1].start()
    grad_ref[...] = (cot.astype(F32) + mm_nt(dpre_ref[...], w_in_ref[...])).astype(BF16)
    outgoing.append(pltpu.make_async_copy(grad_ref, grad_hbm, out_sem.at[4]))
    outgoing[-1].start()
    for copy in outgoing:
        copy.wait()


def layer(lengths, flat, rows, w_in, w_out, cotangent, outputs, after, micro):
    width = w_in.shape[0]
    length = cotangent.shape[1]
    pairs = HEADS // 2
    operands = [lengths, flat, rows, w_in, w_out, cotangent, *outputs, *after]
    shapes = [(length, width), (width, length), (length, 4 * width), (width, length)]
    return pl.pallas_call(
        functools.partial(layer_kernel, micro=micro),
        out_shape=[jax.ShapeDtypeStruct(cotangent.shape, BF16)] + [jax.ShapeDtypeStruct(shape, BF16) for shape in shapes],
        in_specs=[SMEM, VMEM] + [HBM] * (len(operands) - 2),
        out_specs=[HBM] * 5,
        scratch_shapes=[
            pltpu.VMEM(rows.shape, BF16),
            pltpu.VMEM(w_in.shape, BF16),
            pltpu.VMEM(w_out.shape, BF16),
            pltpu.VMEM((length, width), BF16),
            pltpu.VMEM((length, width), BF16),
        ]
        + [pltpu.VMEM(shape, BF16) for shape in shapes]
        + [
            pltpu.VMEM((length, 4 * width), BF16),
            pltpu.VMEM((length, 4 * width), BF16),
            pltpu.VMEM((pairs, length, 2 * length), BF16),
            pltpu.VMEM((pairs, length, 2 * length), BF16),
            pltpu.VMEM((length, width), F32),
            pltpu.VMEM((length, width), BF16),
            pltpu.SemaphoreType.DMA((3,)),
            pltpu.SemaphoreType.DMA((4,)),
            pltpu.SemaphoreType.DMA((5,)),
        ],
        input_output_aliases={6: 0} if outputs else {},
        compiler_params=params(60),
        cost_estimate=cost(8_000_000_000, 6 * 1024 * 1024),
        name=f"layer{micro}",
    )(*operands)


def send_pair_kernel(flat_ref, first_ref, second_ref, out_ref):
    slots = out_ref.shape[0]
    length = first_ref.shape[0]
    places = iota((slots, length), 0)
    one = jnp.where(places == flat_ref[0:1, :], 1.0, 0.0).astype(BF16)
    two = jnp.where(places == flat_ref[1:2, :] + 4, 1.0, 0.0).astype(BF16)
    placing = jnp.concatenate([one, two], axis=1)
    grads = jnp.concatenate([first_ref[...], second_ref[...]], axis=0)
    out_ref[...] = mm(placing, grads).astype(BF16)


def send_pair(flat, first, second, slots):
    return pl.pallas_call(
        send_pair_kernel,
        out_shape=jax.ShapeDtypeStruct((slots, first.shape[1]), BF16),
        grid=(1,),
        in_specs=[pl.BlockSpec(part.shape, lambda i: (0, 0)) for part in (flat, first, second)],
        out_specs=pl.BlockSpec((slots, first.shape[1]), lambda i: (0, 0)),
        compiler_params=params(16),
        cost_estimate=cost(1_000_000_000, 2 * 1024 * 1024),
        name="send_pair",
    )(flat, first, second)


def weights_kernel(half_ref, *refs):
    embs, dpres, gateds, cot_hbm, out_hbm = refs[0:3], refs[3:6], refs[6:9], refs[9], refs[10]
    emb_ref, dpre_ref, gated_ref, cot_ref, out_ref, sem, out_sem = refs[-7:]
    length = cot_hbm.shape[1]
    half = emb_ref.shape[0]
    groups, _, columns = out_ref.shape
    width4 = dpre_ref.shape[1]
    at = pl.ds(pl.multiple_of(half_ref[0] * half, half), half)
    copies = []

    def bring(source, target):
        copy = pltpu.make_async_copy(source, target, sem.at[len(copies)])
        copies.append(copy)
        copy.start()

    for m in range(MB):
        bring(embs[m].at[at], emb_ref.at[:, pl.ds(m * length, length)])
    for group in range(groups):
        first = group * columns
        across = pl.ds(first, min(columns, width4 - first))
        for m in range(MB):
            bring(dpres[m].at[:, across], dpre_ref.at[pl.ds(m * length, length), across])
    for m in range(MB):
        bring(gateds[m].at[at], gated_ref.at[:, pl.ds(m * length, length)])
        bring(cot_hbm.at[m], cot_ref.at[pl.ds(m * length, length)])
    for copy in copies[:MB]:
        copy.wait()
    sends = []
    for group in range(groups):
        first = group * columns
        last = min(first + columns, width4)
        for copy in copies[MB * (group + 1) : MB * (group + 2)]:
            copy.wait()
        out_ref[group, :, : last - first] = mm(emb_ref[...], dpre_ref[:, first:last]).astype(BF16)
        if group == groups - 1:
            for copy in copies[MB * (groups + 1) :]:
                copy.wait()
            out_ref[group, :, last - first :] = mm(gated_ref[...], cot_ref[...]).astype(BF16)
        send = pltpu.make_async_copy(out_ref.at[group], out_hbm.at[group], out_sem.at[group])
        sends.append(send)
        send.start()
    for send in sends:
        send.wait()


def weight_grads(half_index, embs, dpres, gateds, cotangent):
    width, length = embs[0].shape
    width4 = dpres[0].shape[1]
    half = width // 2
    shape = (4, half, (width4 + width) // 4)
    return pl.pallas_call(
        weights_kernel,
        out_shape=jax.ShapeDtypeStruct(shape, BF16),
        in_specs=[SMEM] + [HBM] * 10,
        out_specs=HBM,
        scratch_shapes=[
            pltpu.VMEM((half, MB * length), BF16),
            pltpu.VMEM((MB * length, width4), BF16),
            pltpu.VMEM((half, MB * length), BF16),
            pltpu.VMEM((MB * length, width), BF16),
            pltpu.VMEM(shape, BF16),
            pltpu.SemaphoreType.DMA((7 * MB,)),
            pltpu.SemaphoreType.DMA((4,)),
        ],
        compiler_params=params(60),
        cost_estimate=cost(768 * 512 * 2560, 6 * 1024 * 1024),
        name="weight_grads",
    )(half_index, *embs, *dpres, *gateds, cotangent)


def message_kernel(flat_ref, grad_ref, mine_ref, other_ref, after_ref, out_ref):
    del after_ref
    slots = out_ref.shape[0]
    length, width = grad_ref.shape
    half = width // 2
    places = iota((slots, length), 0)
    one = jnp.where(places == flat_ref[2:3, :], 1.0, 0.0).astype(BF16)
    two = jnp.where(places == flat_ref[2:3, :] + 4, 1.0, 0.0).astype(BF16)
    placing = jnp.concatenate([one, two], axis=1)
    grads = jnp.concatenate([grad_ref[:, :half], grad_ref[:, half:]], axis=0)
    out_ref[:, :half] = mm(placing, grads).astype(BF16)
    out_ref[:, half:] = (mine_ref[...].astype(F32) + other_ref[...].astype(F32)).astype(BF16)


def message(flat, grad, mine, other, after):
    slots, columns = other.shape
    width = grad.shape[1] // 2 + columns
    return pl.pallas_call(
        message_kernel,
        out_shape=jax.ShapeDtypeStruct((slots, width), BF16),
        grid=(1,),
        in_specs=[
            pl.BlockSpec(flat.shape, lambda i: (0, 0)),
            pl.BlockSpec(grad.shape, lambda i: (0, 0)),
            pl.BlockSpec((slots, columns), lambda i: (0, 0)),
            pl.BlockSpec((slots, columns), lambda i: (0, 0)),
            pl.BlockSpec(memory_space=pl.ANY),
        ],
        out_specs=pl.BlockSpec((slots, width), lambda i: (0, 0)),
        compiler_params=params(20),
        cost_estimate=cost(500_000_000, 6 * 1024 * 1024),
        name="message",
    )(flat, grad, mine, other, after)


def shard_sum_kernel(in_ref, out_hbm, copy_ref, sem, *, skip, factor):
    slots = in_ref.shape[0]
    parts = in_ref[:, skip:].astype(F32).reshape(slots // 16, 16, in_ref.shape[1] - skip)
    summed = (jnp.sum(parts, axis=0) * factor).astype(BF16)
    rows = copy_ref.shape[0]
    copy_ref[...] = jnp.broadcast_to(summed[None], (rows // 16, *summed.shape)).reshape(copy_ref.shape)
    copies = [
        pltpu.make_async_copy(copy_ref, out_hbm.at[pl.ds(part * rows, rows)], sem.at[part])
        for part in range(slots // rows)
    ]
    for copy in copies:
        copy.start()
    for copy in copies:
        copy.wait()


def shard_sum(arrived, skip, factor):
    slots = arrived.shape[0]
    columns = arrived.shape[1] - skip
    return pl.pallas_call(
        functools.partial(shard_sum_kernel, skip=skip, factor=factor),
        out_shape=jax.ShapeDtypeStruct((slots, columns), BF16),
        in_specs=[VMEM],
        out_specs=HBM,
        scratch_shapes=[pltpu.VMEM((slots // 4, columns), BF16), pltpu.SemaphoreType.DMA((4,))],
        compiler_params=params(60),
        cost_estimate=cost(1_000_000, 4 * 1024 * 1024),
        name="shard_sum",
    )(arrived)


def table_grad_kernel(pair_row_ref, last_row_ref, pair_ref, last_ref, out_ref, last_rows_ref, *, fold):
    step = pl.program_id(0)
    block = out_ref.shape[0]

    @pl.when(step == 0)
    def _():
        slots = last_ref.shape[0]
        folded = last_ref[:, :fold].astype(F32).reshape(slots // 16, 16, fold)
        even, odd = folded[:, :8], folded[:, 8:]
        top = iota(even.shape, 1) < 4
        left = jnp.where(top, even, pltpu.roll(odd, 4, 1))
        right = jnp.where(top, pltpu.roll(even, 4, 1), odd)
        last_rows_ref[...] = jnp.concatenate([left, right], axis=2).reshape(last_rows_ref.shape).astype(BF16)

    def hot(row):
        places = iota((block, row.shape[1]), 0)
        return jnp.where(places == row - step * block, 1.0, 0.0).astype(BF16)

    out_ref[...] = mm(hot(pair_row_ref[...]), pair_ref[...]) + mm(hot(last_row_ref[...]), last_rows_ref[...])


def table_gradient(pair_row, last_row, pair, last, own_rows):
    width = pair.shape[1]
    steps = 8
    block = own_rows // steps

    def whole(shape):
        return pl.BlockSpec(shape, lambda i: (0,) * len(shape))

    return pl.pallas_call(
        functools.partial(table_grad_kernel, fold=width // 2),
        out_shape=jax.ShapeDtypeStruct((own_rows, width), F32),
        grid=(steps,),
        in_specs=[whole(pair_row.shape), whole(last_row.shape), whole(pair.shape), whole(last.shape)],
        out_specs=pl.BlockSpec((block, width), lambda i: (i, 0)),
        scratch_shapes=[pltpu.VMEM((last_row.shape[1], width), BF16)],
        compiler_params=params(24),
        cost_estimate=cost(2 * own_rows * 1536 * width, 12 * 1024 * 1024),
        name="table_grad",
    )(pair_row, last_row, pair, last)


def finish_kernel(half_ref, in_ref, *rest):
    del half_ref
    win_ref, wout_ref = rest[-2:]
    groups, _, columns = in_ref.shape
    width4 = win_ref.shape[1]
    for group in range(groups):
        first = group * columns
        last = min(first + columns, width4)
        win_ref[:, first:last] = in_ref[group, :, : last - first].astype(F32)
    wout_ref[...] = in_ref[groups - 1, :, width4 - (groups - 1) * columns :].astype(F32)


def finish(half_index, part, before, width, width4):
    half = width // 2
    shape = part.shape
    steps = 2
    return pl.pallas_call(
        finish_kernel,
        out_shape=(jax.ShapeDtypeStruct((width, width4), F32), jax.ShapeDtypeStruct((width, width), F32)),
        grid_spec=pltpu.PrefetchScalarGridSpec(
            num_scalar_prefetch=1,
            grid=(steps,),
            in_specs=[pl.BlockSpec((shape[0], shape[1] // steps, shape[2]), lambda i, which: (0, i, 0))]
            + [pl.BlockSpec(memory_space=pl.ANY)] * len(before),
            out_specs=(
                pl.BlockSpec((half // steps, width4), lambda i, which: (which[0] * steps + i, 0)),
                pl.BlockSpec((half // steps, width), lambda i, which: (which[0] * steps + i, 0)),
            ),
        ),
        input_output_aliases={2: 0, 3: 1} if before else {},
        compiler_params=params(16),
        cost_estimate=cost(1_000_000, 4 * 1024 * 1024),
        name=f"finish{len(before)}",
    )(half_index, part, *before)


def trade(payload):
    return lax.all_to_all(payload, AXES, split_axis=0, concat_axis=0, tiled=True)


def shards(table, w_in, w_out, item_owner, item_slot, seq_lengths, cotangent):
    table_axis = lax.axis_size("table")
    owners_n = lax.axis_size("dp") * table_axis
    length = item_slot.shape[1]
    own_rows, width = table.shape
    slots = owners_n * 8
    core = (lax.axis_index("table") % 2).astype(I32).reshape(1)
    swap = [(i, i ^ 1) for i in range(table_axis)]

    wanted, flat = requests(item_owner.reshape(MB, 1, length), item_slot, owners_n)
    asked = trade(wanted)
    rows_pair = trade(gather(asked, table, 0, 8))
    rows_last = trade(gather(asked, table, 8, 4))
    pair_row = asked[:, :8].reshape(1, slots)
    last_row = asked[:, 8:12].reshape(1, slots // 2)

    out, grad0, emb0, dpre0, gated0 = layer(seq_lengths, flat, rows_pair, w_in, w_out, cotangent, (), (), 0)
    out, grad1, emb1, dpre1, gated1 = layer(seq_lengths, flat, rows_pair, w_in, w_out, cotangent, (out,), (), 1)
    sent_pair = send_pair(flat, grad0, grad1, slots)
    incoming_pair = trade(sent_pair)
    out, grad2, emb2, dpre2, gated2 = layer(
        seq_lengths, flat, rows_last, w_in, w_out, cotangent, (out,), (sent_pair,), 2
    )

    parts = ((emb0, emb1, emb2), (dpre0, dpre1, dpre2), (gated0, gated1, gated2), cotangent)
    sent = weight_grads(1 - core, *parts)
    columns = sent.shape[2]
    sent, incoming_pair = lax.optimization_barrier((sent, incoming_pair))
    other = lax.ppermute(sent.reshape(slots, columns), "table", swap)
    kept = weight_grads(core, *parts)
    arrived = trade(message(flat, grad2, kept.reshape(slots, columns), other, incoming_pair))
    factor = (MB * length * owners_n) ** (-0.5)
    mine_full = trade(shard_sum(arrived, width // 2, factor))
    table_grad = table_gradient(pair_row, last_row, incoming_pair, arrived, own_rows)
    mine_full, table_grad = lax.optimization_barrier((mine_full, table_grad))
    other_full = lax.ppermute(mine_full, "table", swap)
    shape = (4, width // 2, columns)
    partial = finish(core, mine_full.reshape(shape), (), width, w_in.shape[1])
    win_grad, wout_grad = finish(1 - core, other_full.reshape(shape), partial, width, w_in.shape[1])
    return out, table_grad, win_grad, wout_grad


def solution(mesh):
    in_specs = (
        P(AXES, None),
        P(),
        P(),
        P(None, AXES, None),
        P(None, AXES),
        P(None, AXES, None),
        P(None, AXES, None),
    )
    out_specs = (P(None, AXES, None), P(AXES, None), P(), P())
    return jax.shard_map(shards, mesh=mesh, in_specs=in_specs, out_specs=out_specs, check_vma=False)
```

```python
import functools

import jax
import jax.numpy as jnp
from jax import lax
from jax.experimental import pallas as pl
from jax.experimental.pallas import tpu as pltpu
from jax.sharding import PartitionSpec as P

HEADS = 8
MB = 3
CAP = 4
AXES = ("dp", "table")
F32 = jnp.float32
BF16 = jnp.bfloat16
I32 = jnp.int32
VMEM = pl.BlockSpec(memory_space=pltpu.VMEM)
HBM = pl.BlockSpec(memory_space=pltpu.HBM)
SMEM = pl.BlockSpec(memory_space=pltpu.SMEM)


def iota(shape, dim):
    return lax.broadcasted_iota(I32, shape, dim)


def mm(a, b):
    return jnp.dot(a, b, preferred_element_type=F32)


def mm_nt(a, b):
    return lax.dot_general(a, b, (((1,), (1,)), ((), ())), preferred_element_type=F32)


def mm_tn(a, b):
    return lax.dot_general(a, b, (((0,), (0,)), ((), ())), preferred_element_type=F32)


def params(mib):
    return pltpu.CompilerParams(vmem_limit_bytes=mib * 1024 * 1024)


def cost(flops, bytes_accessed):
    return pl.CostEstimate(flops=flops, bytes_accessed=bytes_accessed, transcendentals=0)


def request_kernel(owner_ref, slot_ref, wanted_ref, flat_ref):
    length = slot_ref.shape[1]
    owners_n = wanted_ref.shape[0]
    upto = (iota((length, length), 0) <= iota((length, length), 1)).astype(BF16)
    lane_row = iota((128, length), 0)
    high = jnp.zeros((owners_n, 128), F32)
    low = jnp.zeros((owners_n, 128), F32)
    live = jnp.zeros((owners_n, 128), F32)
    flat_ref[...] = jnp.zeros(flat_ref.shape, I32)
    for micro in range(MB):
        owner = owner_ref[micro]
        slot = slot_ref[micro : micro + 1, :]
        hot = (iota((owners_n, length), 0) == owner).astype(F32)
        hot_bf = hot.astype(BF16)
        counts = mm(hot_bf, upto)
        rank = (jnp.sum(counts * hot, axis=0, keepdims=True) - 1.0).astype(I32)
        flat_ref[micro : micro + 1, :] = owner * 8 + rank
        here = lane_row == rank + CAP * micro
        high = high + mm_nt(hot_bf, jnp.where(here, (slot >> 6).astype(F32), 0.0).astype(BF16))
        low = low + mm_nt(hot_bf, jnp.where(here, (slot & 63).astype(F32), 0.0).astype(BF16))
        live = live + mm_nt(hot_bf, jnp.where(here, 1.0, 0.0).astype(BF16))
    wanted_ref[...] = jnp.where(live > 0.5, high * 64.0 + low, -1.0).astype(I32)


def requests(owner, slot, owners_n):
    return pl.pallas_call(
        request_kernel,
        out_shape=(
            jax.ShapeDtypeStruct((owners_n, 128), I32),
            jax.ShapeDtypeStruct((8, slot.shape[1]), I32),
        ),
        grid=(1,),
        in_specs=[
            pl.BlockSpec(owner.shape, lambda i: (0, 0, 0)),
            pl.BlockSpec(slot.shape, lambda i: (0, 0)),
        ],
        out_specs=(
            pl.BlockSpec((owners_n, 128), lambda i: (0, 0)),
            pl.BlockSpec((8, slot.shape[1]), lambda i: (0, 0)),
        ),
        compiler_params=params(8),
        name="requests",
    )(owner, slot)


def unfold(folded):
    half = folded.shape[1]
    whole = folded.reshape(folded.shape[0] // 16, 16, half)
    even, odd = whole[:, :8], whole[:, 8:]
    top = iota(even.shape, 1) < 4
    left = jnp.where(top, even, pltpu.roll(odd, 4, 1))
    right = jnp.where(top, pltpu.roll(even, 4, 1), odd)
    return jnp.concatenate([left, right], axis=2).reshape(folded.shape[0] // 2, 2 * half)


def gather_kernel(asked_hbm, table_hbm, out_ref, asked_ref, block_ref, wide_ref, sem):
    steps, block, columns = block_ref.shape
    devices = asked_ref.shape[0]
    copies = [pltpu.make_async_copy(asked_hbm, asked_ref, sem.at[steps])]
    for step in range(steps):
        source = table_hbm.at[pl.ds(step * block, block)]
        copies.append(pltpu.make_async_copy(source, block_ref.at[step], sem.at[step]))
    for copy in copies:
        copy.start()
    for step in range(steps):
        copies[1 + step].wait()
        wide_ref[step * block : (step + 1) * block, :] = block_ref[step].astype(F32)
    copies[0].wait()
    half = columns // 2
    below = iota((8, columns), 0)
    below_half = iota((8, half), 0)

    def two_devices(turn, carry):
        pairs = []
        lasts = []
        for which in range(2):
            names = [jnp.maximum(asked_ref[2 * turn + which, place], 0) for place in range(12)]
            rows = [wide_ref[pl.ds(name, 1), :] for name in names]
            tile = jnp.broadcast_to(rows[0], (8, columns))
            for place in range(1, 8):
                tile = jnp.where(below == place, rows[place], tile)
            pairs.append(tile)
            parts = [row[:, :half] for row in rows[8:]] + [row[:, half:] for row in rows[8:]]
            tile = jnp.broadcast_to(parts[0], (8, half))
            for place in range(1, 8):
                tile = jnp.where(below_half == place, parts[place], tile)
            lasts.append(tile)
        at = pl.ds(pl.multiple_of(16 * turn, 16), 16)
        out_ref[at, :columns] = jnp.concatenate(pairs, axis=0).astype(BF16)
        out_ref[at, columns:] = jnp.concatenate(lasts, axis=0).astype(BF16)
        return carry

    lax.fori_loop(0, devices // 2, two_devices, 0)


def gather(asked, table):
    own_rows, columns = table.shape
    devices = asked.shape[0]
    steps = 8
    return pl.pallas_call(
        gather_kernel,
        out_shape=jax.ShapeDtypeStruct((devices * 8, columns + columns // 2), BF16),
        in_specs=[HBM, HBM],
        out_specs=VMEM,
        scratch_shapes=[
            pltpu.SMEM(asked.shape, I32),
            pltpu.VMEM((steps, own_rows // steps, columns), BF16),
            pltpu.VMEM((own_rows, columns), F32),
            pltpu.SemaphoreType.DMA((steps + 1,)),
        ],
        compiler_params=params(59),
        cost_estimate=cost(6_000_000_000, 6 * 1024 * 1024),
        name="gather",
    )(asked, table)


def column_of(row, copies=128):
    return jnp.transpose(jnp.broadcast_to(row.astype(F32), (copies, row.shape[1])))


def layer_body(micro, lengths_ref, column, rows_ref, weights, cot, stores, scratch, folded):
    w_in_ref, w_out_ref, wait_in, wait_out = weights
    out_ref, grad_ref, emb_t_ref, gated_t_ref, dpre_ref, stored = stores
    hidden_ref, slope_ref, weight_ref, dsilu_ref, att_ref, datt_ref = scratch
    width = w_out_ref.shape[0]
    length = hidden_ref.shape[0]
    slots = rows_ref.shape[0]
    chunk = 512

    def placing(shift):
        lanes = iota((length, 128), 1).astype(F32)
        parts = [
            jnp.where(column == lanes + float(first - shift), 1.0, 0.0).astype(BF16)
            for first in range(0, slots, 128)
        ]
        return jnp.concatenate(parts, axis=1)

    if folded:
        places = (placing(0), placing(4))
        rows = rows_ref[:, width:]
        embedded = jnp.concatenate([mm(places[0], rows), mm(places[1], rows)], axis=1)
    else:
        places = placing(4 * micro)
        embedded = mm(places, rows_ref[:, :width])
    emb_t_ref[...] = jnp.transpose(embedded).astype(BF16)
    stored("emb_t")
    emb = embedded.astype(BF16)

    for which, first in enumerate(range(0, 4 * width, chunk)):
        wait_in(which)
        at = slice(first, first + chunk)
        half = mm(emb, w_in_ref[:, at]) * 0.5
        tanh = jnp.tanh(half)
        act = half + half * tanh
        hidden_ref[:, at] = act.astype(BF16)
        slope_ref[:, at] = (0.5 * ((1.0 + tanh) + act * (1.0 - tanh))).astype(BF16)

    ends = []
    total = 0
    for which in range(3):
        total = total + lengths_ref[micro, 0, which]
        ends.append(total)

    def segment(places):
        return sum((places >= end).astype(I32) for end in ends)

    query_at = iota((length, length), 0)
    key_at = iota((length, length), 1)
    allowed = (segment(query_at) == segment(key_at)) & (key_at <= query_at)

    lane = iota((1, 128), 1)
    first_head = (lane < 64).astype(F32)
    second_head = 1.0 - first_head
    masks = (first_head.astype(BF16), second_head.astype(BF16))
    score_masks = ((first_head * 0.0625).astype(BF16), (second_head * 0.0625).astype(BF16))
    pairs = HEADS // 2
    for pair in range(pairs):
        lanes = slice(128 * pair, 128 * pair + 128)
        value = hidden_ref[:, width + 128 * pair : width + 128 * pair + 128]
        query = hidden_ref[:, 2 * width + 128 * pair : 2 * width + 128 * pair + 128]
        key = hidden_ref[:, 3 * width + 128 * pair : 3 * width + 128 * pair + 128]
        for head in range(2):
            half = mm_nt(query * score_masks[head], key)
            tanh = jnp.tanh(half)
            act = half + half * tanh
            at = slice(length * head, length * head + length)
            weight_ref[pair, :, at] = jnp.where(allowed, act, 0.0).astype(BF16)
            dsilu_ref[pair, :, at] = jnp.where(
                allowed, (1.0 + tanh) + act * (1.0 - tanh), 0.0
            ).astype(BF16)
        both = jnp.concatenate([value * masks[0], value * masks[1]], axis=0)
        att_ref[:, lanes] = mm(weight_ref[pair], both)

    attended = att_ref[...]
    centred = attended - jnp.mean(attended, axis=1, keepdims=True)
    inverse = lax.rsqrt(jnp.mean(centred * centred, axis=1, keepdims=True) + 1e-05)
    normed = centred * inverse
    gate = hidden_ref[:, :width].astype(F32)
    gated = normed * gate
    gated_t_ref[...] = jnp.transpose(gated).astype(BF16)
    stored("gated_t")
    wait_out()
    cot = cot()
    out_ref[...] = (embedded + mm(gated.astype(BF16), w_out_ref[...])).astype(BF16)
    stored("out")

    dgated = mm_nt(cot, w_out_ref[...])
    dgate = dgated * normed
    dnormed = dgated * gate
    dpre_ref[:, :width] = (dgate * slope_ref[:, :width].astype(F32)).astype(BF16)
    shared = jnp.mean(dnormed * normed, axis=1, keepdims=True)
    dcentred = inverse * (dnormed - normed * shared)
    datt = dcentred - jnp.mean(dcentred, axis=1, keepdims=True)
    datt_ref[...] = datt.astype(BF16)

    for pair in range(pairs):
        at_value = slice(width + 128 * pair, width + 128 * pair + 128)
        at_query = slice(2 * width + 128 * pair, 2 * width + 128 * pair + 128)
        at_key = slice(3 * width + 128 * pair, 3 * width + 128 * pair + 128)
        value = hidden_ref[:, at_value]
        query = hidden_ref[:, at_query]
        key = hidden_ref[:, at_key]
        dhead = datt_ref[:, 128 * pair : 128 * pair + 128]
        parts = []
        for head in range(2):
            at = slice(length * head, length * head + length)
            dweight = mm_nt(dhead * masks[head], value)
            parts.append((dweight * dsilu_ref[pair, :, at].astype(F32)).astype(BF16))
        dscore = jnp.concatenate(parts, axis=1)
        both_keys = jnp.concatenate([key * score_masks[0], key * score_masks[1]], axis=0)
        dquery = mm(dscore, both_keys)
        dkeys = mm_tn(dscore, query * jnp.asarray(0.0625, BF16))
        dkey = jnp.where(lane < 64, dkeys[:length], dkeys[length:])
        dvalues = mm_tn(weight_ref[pair], dhead)
        dvalue = jnp.where(lane < 64, dvalues[:length], dvalues[length:])
        for at, grad in ((at_value, dvalue), (at_query, dquery), (at_key, dkey)):
            dpre_ref[:, at] = (grad * slope_ref[:, at].astype(F32)).astype(BF16)

    stored("dpre")
    grad_ref[...] = (cot.astype(F32) + mm_nt(dpre_ref[...], w_in_ref[...])).astype(BF16)


def start_all(pairs, sem):
    copies = [pltpu.make_async_copy(source, target, sem.at[k]) for k, (source, target) in enumerate(pairs)]
    for copy in copies:
        copy.start()
    return copies


def waiting(copies):
    pending = list(copies)

    def wait():
        while pending:
            pending.pop().wait()

    return wait


def column_chunks(source, target, chunk):
    at = [pl.ds(first, chunk) for first in range(0, source.shape[1], chunk)]
    return [(source.at[:, here], target.at[:, here]) for here in at]


def layer_scratch(length, width):
    pairs = HEADS // 2
    return [
        pltpu.VMEM((length, 4 * width), BF16),
        pltpu.VMEM((length, 4 * width), BF16),
        pltpu.VMEM((pairs, length, 2 * length), BF16),
        pltpu.VMEM((pairs, length, 2 * length), BF16),
        pltpu.VMEM((length, width), F32),
        pltpu.VMEM((length, width), BF16),
    ]


def layers_kernel(half_ref, lengths_ref, flat_ref, rows_ref, w_in_hbm, w_out_hbm, cot_hbm, *rest):
    out_hbm, sent_hbm, back_hbm, kept_ref = rest[:4]
    w_in_ref, w_out_ref, cot_ref, out_ref, emb_t_ref, gated_t_ref, dpre_ref, grad_ref, sent_ref, back_ref = rest[4:14]
    scratch, (in_sem, out_sem) = rest[14:20], rest[20:]
    slots = rows_ref.shape[0]
    width = w_out_ref.shape[0]
    length = cot_hbm.shape[1]
    width4 = w_in_ref.shape[1]
    w_chunks = column_chunks(w_in_hbm, w_in_ref, 512)
    at = [pl.ds(m * length, length) for m in range(MB)]
    copies = start_all(
        [*w_chunks, (w_out_hbm, w_out_ref)] + [(cot_hbm.at[m], cot_ref.at[at[m]]) for m in range(MB)], in_sem
    )
    waits = [waiting([copy]) for copy in copies]
    outgoing = []

    def send(source, target):
        outgoing.append(pltpu.make_async_copy(source, target, out_sem.at[len(outgoing)]))
        outgoing[-1].start()

    for micro in range(MB):

        def stored(name, micro=micro):
            if name == "out":
                send(out_ref.at[micro], out_hbm.at[micro])

        def cot(micro=micro):
            waits[5 + micro]()
            return cot_ref[micro * length : (micro + 1) * length]

        layer_body(
            micro,
            lengths_ref,
            column_of(flat_ref[micro : micro + 1, :]),
            rows_ref,
            (w_in_ref, w_out_ref, lambda which: waits[which](), waits[4]),
            cot,
            (
                out_ref.at[micro],
                grad_ref.at[at[micro]],
                emb_t_ref.at[:, at[micro]],
                gated_t_ref.at[:, at[micro]],
                dpre_ref.at[at[micro]],
                stored,
            ),
            scratch,
            micro == 2,
        )
    groups, half, columns = sent_ref.shape

    def weights(mine, put):
        rows = pl.ds(pl.multiple_of(mine * half, half), half)
        for group in range(groups):
            first = group * columns
            last = min(first + columns, width4)
            part = mm(emb_t_ref[rows, :], dpre_ref[:, first:last]).astype(BF16)
            if group == groups - 1:
                part = jnp.concatenate([part, mm(gated_t_ref[rows, :], cot_ref[...]).astype(BF16)], axis=1)
            put(group, part)

    def put_sent(group, part):
        sent_ref[group] = part
        send(sent_ref.at[group], sent_hbm.at[group])

    def put_kept(group, part):
        kept_ref[group * half : (group + 1) * half, :] = part

    weights(1 - half_ref[0], put_sent)
    places = iota((slots, length), 0)

    def placing(micro, shift):
        return jnp.where(places == flat_ref[micro : micro + 1, :] + shift, 1.0, 0.0).astype(BF16)

    pair = jnp.concatenate([placing(0, 0), placing(1, 4)], axis=1)
    back_ref[:, :width] = mm(pair, grad_ref[: 2 * length]).astype(BF16)
    last = jnp.concatenate([placing(2, 0), placing(2, 4)], axis=1)
    halves = [grad_ref[2 * length :, : width // 2], grad_ref[2 * length :, width // 2 :]]
    back_ref[:, width:] = mm(last, jnp.concatenate(halves, axis=0)).astype(BF16)
    send(back_ref, back_hbm)
    weights(half_ref[0], put_kept)
    for copy in outgoing:
        copy.wait()


def layers(core, lengths, flat, rows, w_in, w_out, cotangent):
    width = w_in.shape[0]
    length = cotangent.shape[1]
    slots = rows.shape[0]
    columns = 5 * width // 4
    sent = (4, width // 2, columns)
    return pl.pallas_call(
        layers_kernel,
        out_shape=[
            jax.ShapeDtypeStruct(shape, BF16) for shape in [cotangent.shape, sent, rows.shape, (slots, columns)]
        ],
        in_specs=[SMEM, SMEM, VMEM, VMEM] + [HBM] * 3,
        out_specs=[HBM, HBM, HBM, VMEM],
        scratch_shapes=[
            pltpu.VMEM(shape, BF16)
            for shape in [
                w_in.shape,
                w_out.shape,
                (MB * length, width),
                cotangent.shape,
                (width, MB * length),
                (width, MB * length),
                (MB * length, 4 * width),
                (MB * length, width),
                sent,
                rows.shape,
            ]
        ]
        + layer_scratch(length, width)
        + [pltpu.SemaphoreType.DMA((8,)), pltpu.SemaphoreType.DMA((8,))],
        compiler_params=params(46),
        cost_estimate=cost(28_000_000_000, 10 * 1024 * 1024),
        name="layers",
    )(core, lengths, flat, rows, w_in, w_out, cotangent)


def message_kernel(back_hbm, kept_ref, other_ref, out_ref, sem):
    skip = back_hbm.shape[1]
    copy = pltpu.make_async_copy(back_hbm, out_ref.at[:, pl.ds(0, skip)], sem)
    copy.start()
    out_ref[:, skip:] = (kept_ref[...].astype(F32) + other_ref[...].astype(F32)).astype(BF16)
    copy.wait()


def message(back, kept, other):
    return pl.pallas_call(
        message_kernel,
        out_shape=jax.ShapeDtypeStruct((back.shape[0], back.shape[1] + kept.shape[1]), BF16),
        in_specs=[HBM, VMEM, VMEM],
        out_specs=VMEM,
        scratch_shapes=[pltpu.SemaphoreType.DMA],
        compiler_params=params(16),
        cost_estimate=cost(1_000_000, 4 * 1024 * 1024),
        name="message",
    )(back, kept, other)


def shard_sum_kernel(in_ref, out_ref, *, skip, factor):
    slots = in_ref.shape[0]
    parts = in_ref[:, skip:].astype(F32).reshape(slots // 16, 16, in_ref.shape[1] - skip)
    summed = (jnp.sum(parts, axis=0) * factor).astype(BF16)
    out_ref[...] = jnp.broadcast_to(summed[None], (slots // 16, *summed.shape)).reshape(out_ref.shape)


def shard_sum(arrived, skip, factor):
    slots = arrived.shape[0]
    return pl.pallas_call(
        functools.partial(shard_sum_kernel, skip=skip, factor=factor),
        out_shape=jax.ShapeDtypeStruct((slots, arrived.shape[1] - skip), BF16),
        in_specs=[VMEM],
        out_specs=VMEM,
        compiler_params=params(16),
        cost_estimate=cost(1_000_000, 4 * 1024 * 1024),
        name="shard_sum",
    )(arrived)


def table_grad_kernel(pair_row_ref, last_row_ref, arrived_ref, out_ref, last_rows_ref):
    step = pl.program_id(0)
    block, width = out_ref.shape

    @pl.when(step == 0)
    def _():
        last_rows_ref[...] = unfold(arrived_ref[:, width : width + width // 2].astype(F32)).astype(BF16)

    def hot(row):
        places = iota((block, row.shape[1]), 0)
        return jnp.where(places == row - step * block, 1.0, 0.0).astype(BF16)

    out_ref[...] = mm(hot(pair_row_ref[...]), arrived_ref[:, :width]) + mm(
        hot(last_row_ref[...]), last_rows_ref[...]
    )


def table_gradient(pair_row, last_row, arrived, own_rows, width):
    steps = 8
    block = own_rows // steps

    def whole(shape):
        return pl.BlockSpec(shape, lambda i: (0,) * len(shape))

    return pl.pallas_call(
        table_grad_kernel,
        out_shape=jax.ShapeDtypeStruct((own_rows, width), F32),
        grid=(steps,),
        in_specs=[whole(pair_row.shape), whole(last_row.shape), whole(arrived.shape)],
        out_specs=pl.BlockSpec((block, width), lambda i: (i, 0)),
        scratch_shapes=[pltpu.VMEM((last_row.shape[1], width), BF16)],
        compiler_params=params(24),
        cost_estimate=cost(2 * own_rows * 1536 * width, 12 * 1024 * 1024),
        name="table_grad",
    )(pair_row, last_row, arrived)


def finish_kernel(half_ref, in_ref, *rest):
    del half_ref
    win_ref, wout_ref = rest[-2:]
    groups, _, columns = in_ref.shape
    width4 = win_ref.shape[1]
    for group in range(groups):
        first = group * columns
        last = min(first + columns, width4)
        win_ref[:, first:last] = in_ref[group, :, : last - first].astype(F32)
    wout_ref[...] = in_ref[groups - 1, :, width4 - (groups - 1) * columns :].astype(F32)


def finish(half_index, part, before, width, width4):
    half = width // 2
    shape = part.shape
    steps = 2
    return pl.pallas_call(
        finish_kernel,
        out_shape=(jax.ShapeDtypeStruct((width, width4), F32), jax.ShapeDtypeStruct((width, width), F32)),
        grid_spec=pltpu.PrefetchScalarGridSpec(
            num_scalar_prefetch=1,
            grid=(steps,),
            in_specs=[pl.BlockSpec((shape[0], shape[1] // steps, shape[2]), lambda i, which: (0, i, 0))]
            + [pl.BlockSpec(memory_space=pl.ANY)] * len(before),
            out_specs=(
                pl.BlockSpec((half // steps, width4), lambda i, which: (which[0] * steps + i, 0)),
                pl.BlockSpec((half // steps, width), lambda i, which: (which[0] * steps + i, 0)),
            ),
        ),
        input_output_aliases={2: 0, 3: 1} if before else {},
        compiler_params=params(16),
        cost_estimate=cost(1_000_000, 4 * 1024 * 1024),
        name=f"finish{len(before)}",
    )(half_index, part, *before)


def trade(payload):
    return lax.all_to_all(payload, AXES, split_axis=0, concat_axis=0, tiled=True)


def shards(table, w_in, w_out, item_owner, item_slot, seq_lengths, cotangent):
    table_axis = lax.axis_size("table")
    owners_n = lax.axis_size("dp") * table_axis
    length = item_slot.shape[1]
    own_rows, width = table.shape
    slots = owners_n * 8
    core = (lax.axis_index("table") % 2).astype(I32).reshape(1)
    swap = [(i, i ^ 1) for i in range(table_axis)]

    wanted, flat = requests(item_owner.reshape(MB, 1, length), item_slot, owners_n)
    asked = trade(wanted)
    rows = trade(gather(asked, table))
    pair_row = asked[:, :8].reshape(1, slots)
    last_row = asked[:, 8:12].reshape(1, slots // 2)
    out, sent, back, kept = layers(core, seq_lengths, flat, rows, w_in, w_out, cotangent)
    columns = sent.shape[2]
    other = lax.ppermute(sent.reshape(slots, columns), "table", swap)
    arrived = trade(message(back, kept, other))
    factor = (MB * length * owners_n) ** (-0.5)
    mine_full = trade(shard_sum(arrived, rows.shape[1], factor))
    table_grad = table_gradient(pair_row, last_row, arrived, own_rows, width)
    mine_full, table_grad = lax.optimization_barrier((mine_full, table_grad))
    other_full = lax.ppermute(mine_full, "table", swap)
    shape = (4, width // 2, columns)
    partial = finish(core, mine_full.reshape(shape), (), width, w_in.shape[1])
    win_grad, wout_grad = finish(1 - core, other_full.reshape(shape), partial, width, w_in.shape[1])
    return out, table_grad, win_grad, wout_grad


def solution(mesh):
    in_specs = (
        P(AXES, None),
        P(),
        P(),
        P(None, AXES, None),
        P(None, AXES),
        P(None, AXES, None),
        P(None, AXES, None),
    )
    out_specs = (P(None, AXES, None), P(AXES, None), P(), P())
    return jax.shard_map(shards, mesh=mesh, in_specs=in_specs, out_specs=out_specs, check_vma=False)
```

```python
import functools

import jax
import jax.numpy as jnp
from jax import lax
from jax.experimental import pallas as pl
from jax.experimental.pallas import tpu as pltpu
from jax.sharding import PartitionSpec as P

HEADS = 8
MB = 3
CAP = 4
AXES = ("dp", "table")
F32 = jnp.float32
BF16 = jnp.bfloat16
I32 = jnp.int32
VMEM = pl.BlockSpec(memory_space=pltpu.VMEM)
HBM = pl.BlockSpec(memory_space=pltpu.HBM)
SMEM = pl.BlockSpec(memory_space=pltpu.SMEM)


def iota(shape, dim):
    return lax.broadcasted_iota(I32, shape, dim)


def mm(a, b):
    return jnp.dot(a, b, preferred_element_type=F32)


def mm_nt(a, b):
    return lax.dot_general(a, b, (((1,), (1,)), ((), ())), preferred_element_type=F32)


def mm_tn(a, b):
    return lax.dot_general(a, b, (((0,), (0,)), ((), ())), preferred_element_type=F32)


def params(mib):
    return pltpu.CompilerParams(vmem_limit_bytes=mib * 1024 * 1024)


def cost(flops, bytes_accessed):
    return pl.CostEstimate(flops=flops, bytes_accessed=bytes_accessed, transcendentals=0)


def request_kernel(owner_ref, slot_ref, wanted_ref, flat_ref):
    length = slot_ref.shape[1]
    owners_n = wanted_ref.shape[0]
    upto = (iota((length, length), 0) <= iota((length, length), 1)).astype(BF16)
    lane_row = iota((128, length), 0)
    high = jnp.zeros((owners_n, 128), F32)
    low = jnp.zeros((owners_n, 128), F32)
    live = jnp.zeros((owners_n, 128), F32)
    flat_ref[...] = jnp.zeros(flat_ref.shape, I32)
    for micro in range(MB):
        owner = owner_ref[micro]
        slot = slot_ref[micro : micro + 1, :]
        hot = (iota((owners_n, length), 0) == owner).astype(F32)
        hot_bf = hot.astype(BF16)
        counts = mm(hot_bf, upto)
        rank = (jnp.sum(counts * hot, axis=0, keepdims=True) - 1.0).astype(I32)
        flat_ref[micro : micro + 1, :] = owner * 8 + rank
        here = lane_row == rank + CAP * micro
        high = high + mm_nt(hot_bf, jnp.where(here, (slot >> 6).astype(F32), 0.0).astype(BF16))
        low = low + mm_nt(hot_bf, jnp.where(here, (slot & 63).astype(F32), 0.0).astype(BF16))
        live = live + mm_nt(hot_bf, jnp.where(here, 1.0, 0.0).astype(BF16))
    wanted_ref[...] = jnp.where(live > 0.5, high * 64.0 + low, -1.0).astype(I32)


def requests(owner, slot, owners_n):
    return pl.pallas_call(
        request_kernel,
        out_shape=(
            jax.ShapeDtypeStruct((owners_n, 128), I32),
            jax.ShapeDtypeStruct((8, slot.shape[1]), I32),
        ),
        grid=(1,),
        in_specs=[
            pl.BlockSpec(owner.shape, lambda i: (0, 0, 0)),
            pl.BlockSpec(slot.shape, lambda i: (0, 0)),
        ],
        out_specs=(
            pl.BlockSpec((owners_n, 128), lambda i: (0, 0)),
            pl.BlockSpec((8, slot.shape[1]), lambda i: (0, 0)),
        ),
        compiler_params=params(8),
        name="requests",
    )(owner, slot)


def unfold(folded):
    half = folded.shape[1]
    whole = folded.reshape(folded.shape[0] // 16, 16, half)
    even, odd = whole[:, :8], whole[:, 8:]
    top = iota(even.shape, 1) < 4
    left = jnp.where(top, even, pltpu.roll(odd, 4, 1))
    right = jnp.where(top, pltpu.roll(even, 4, 1), odd)
    return jnp.concatenate([left, right], axis=2).reshape(folded.shape[0] // 2, 2 * half)


def gather_kernel(asked_hbm, table_hbm, out_ref, asked_ref, block_ref, wide_ref, sem):
    steps, block, columns = block_ref.shape
    devices = asked_ref.shape[0]
    copies = [pltpu.make_async_copy(asked_hbm, asked_ref, sem.at[steps])]
    for step in range(steps):
        source = table_hbm.at[pl.ds(step * block, block)]
        copies.append(pltpu.make_async_copy(source, block_ref.at[step], sem.at[step]))
    for copy in copies:
        copy.start()
    for step in range(steps):
        copies[1 + step].wait()
        wide_ref[step * block : (step + 1) * block, :] = block_ref[step].astype(F32)
    copies[0].wait()
    half = columns // 2
    below = iota((8, columns), 0)
    below_half = iota((8, half), 0)

    def two_devices(turn, carry):
        pairs = []
        lasts = []
        for which in range(2):
            names = [jnp.maximum(asked_ref[2 * turn + which, place], 0) for place in range(12)]
            rows = [wide_ref[pl.ds(name, 1), :] for name in names]
            tile = jnp.broadcast_to(rows[0], (8, columns))
            for place in range(1, 8):
                tile = jnp.where(below == place, rows[place], tile)
            pairs.append(tile)
            parts = [row[:, :half] for row in rows[8:]] + [row[:, half:] for row in rows[8:]]
            tile = jnp.broadcast_to(parts[0], (8, half))
            for place in range(1, 8):
                tile = jnp.where(below_half == place, parts[place], tile)
            lasts.append(tile)
        at = pl.ds(pl.multiple_of(16 * turn, 16), 16)
        out_ref[at, :columns] = jnp.concatenate(pairs, axis=0).astype(BF16)
        out_ref[at, columns:] = jnp.concatenate(lasts, axis=0).astype(BF16)
        return carry

    lax.fori_loop(0, devices // 2, two_devices, 0)


def gather(asked, table):
    own_rows, columns = table.shape
    devices = asked.shape[0]
    steps = 8
    return pl.pallas_call(
        gather_kernel,
        out_shape=jax.ShapeDtypeStruct((devices * 8, columns + columns // 2), BF16),
        in_specs=[HBM, HBM],
        out_specs=VMEM,
        scratch_shapes=[
            pltpu.SMEM(asked.shape, I32),
            pltpu.VMEM((steps, own_rows // steps, columns), BF16),
            pltpu.VMEM((own_rows, columns), F32),
            pltpu.SemaphoreType.DMA((steps + 1,)),
        ],
        compiler_params=params(59),
        cost_estimate=cost(6_000_000_000, 6 * 1024 * 1024),
        name="gather",
    )(asked, table)


def column_of(row, copies=128):
    return jnp.transpose(jnp.broadcast_to(row.astype(F32), (copies, row.shape[1])))


def both_heads(pair_columns, masks):
    return jnp.concatenate([pair_columns * masks[0], pair_columns * masks[1]], axis=0)


def layers_kernel(half_ref, lengths_ref, flat_ref, rows_ref, w_in_hbm, w_out_hbm, cot_hbm, *rest):
    out_hbm, sent_hbm, back_hbm, kept_ref = rest[:4]
    w_in_ref, w_out_ref, cot_ref, out_ref, emb_t_ref, gated_t_ref, dpre_ref, grad_ref, sent_ref, back_ref = rest[4:14]
    emb_ref, hidden_ref, slope_ref, weight_ref, dsilu_ref, att_ref, datt_ref, in_sem, out_sem = rest[14:]
    slots = rows_ref.shape[0]
    width = w_out_ref.shape[0]
    length = cot_hbm.shape[1]
    width4 = w_in_ref.shape[1]
    chunk = 512
    chunks = [slice(first, first + chunk) for first in range(0, width4, chunk)]
    incoming = []

    def bring(source, target):
        incoming.append(pltpu.make_async_copy(source, target, in_sem.at[len(incoming)]))
        incoming[-1].start()

    for part in chunks:
        at = pl.ds(part.start, chunk)
        bring(w_in_hbm.at[:, at], w_in_ref.at[:, at])
    bring(w_out_hbm, w_out_ref)
    bring(cot_hbm, cot_ref)
    outgoing = []

    def send(source, target):
        outgoing.append(pltpu.make_async_copy(source, target, out_sem.at[len(outgoing)]))
        outgoing[-1].start()

    of = [slice(micro * length, (micro + 1) * length) for micro in range(MB)]
    for micro in range(MB):
        column = column_of(flat_ref[micro : micro + 1, :])

        def placed(shift, column=column):
            lanes = iota((length, 128), 1).astype(F32)
            parts = [
                jnp.where(column == lanes + float(first - shift), 1.0, 0.0).astype(BF16)
                for first in range(0, slots, 128)
            ]
            return jnp.concatenate(parts, axis=1)

        if micro == 2:
            rows = rows_ref[:, width:]
            embedded = jnp.concatenate([mm(placed(0), rows), mm(placed(4), rows)], axis=1)
        else:
            embedded = mm(placed(4 * micro), rows_ref[:, :width])
        emb_ref[of[micro], :] = embedded.astype(BF16)
        emb_t_ref[:, of[micro]] = jnp.transpose(embedded).astype(BF16)

    for which, at in enumerate(chunks):
        incoming[which].wait()
        half = mm(emb_ref[...], w_in_ref[:, at]) * 0.5
        tanh = jnp.tanh(half)
        act = half + half * tanh
        hidden_ref[:, at] = act.astype(BF16)
        slope_ref[:, at] = (0.5 * ((1.0 + tanh) + act * (1.0 - tanh))).astype(BF16)

    lane = iota((1, 128), 1)
    first_head = (lane < 64).astype(F32)
    second_head = 1.0 - first_head
    masks = (first_head.astype(BF16), second_head.astype(BF16))
    score_masks = ((first_head * 0.0625).astype(BF16), (second_head * 0.0625).astype(BF16))
    pairs = HEADS // 2
    query_at = iota((length, length), 0)
    key_at = iota((length, length), 1)
    for micro in range(MB):
        ends = []
        total = 0
        for which in range(3):
            total = total + lengths_ref[micro, 0, which]
            ends.append(total)

        def segment(places, ends=ends):
            return sum((places >= end).astype(I32) for end in ends)

        allowed = (segment(query_at) == segment(key_at)) & (key_at <= query_at)
        for pair in range(pairs):
            first = 128 * pair
            value = hidden_ref[of[micro], width + first : width + first + 128]
            query = hidden_ref[of[micro], 2 * width + first : 2 * width + first + 128]
            key = hidden_ref[of[micro], 3 * width + first : 3 * width + first + 128]
            halves = mm_nt(both_heads(query, score_masks), key)
            for head in range(2):
                at = slice(length * head, length * head + length)
                half = halves[at]
                tanh = jnp.tanh(half)
                act = half + half * tanh
                weight_ref[micro * pairs + pair, :, at] = jnp.where(allowed, act, 0.0).astype(BF16)
                dsilu_ref[micro * pairs + pair, :, at] = jnp.where(
                    allowed, (1.0 + tanh) + act * (1.0 - tanh), 0.0
                ).astype(BF16)
            att_ref[of[micro], first : first + 128] = mm(
                weight_ref[micro * pairs + pair], both_heads(value, masks)
            )

    incoming[-2].wait()
    incoming[-1].wait()
    cot = cot_ref[...].reshape(MB * length, width)
    dgated_all = mm_nt(cot, w_out_ref[...])
    gated_all = []
    for micro in range(MB):
        attended = att_ref[of[micro], :]
        centred = attended - jnp.mean(attended, axis=1, keepdims=True)
        inverse = lax.rsqrt(jnp.mean(centred * centred, axis=1, keepdims=True) + 1e-05)
        normed = centred * inverse
        gate = hidden_ref[of[micro], :width].astype(F32)
        gated = normed * gate
        gated_t_ref[:, of[micro]] = jnp.transpose(gated).astype(BF16)
        gated_all.append(gated.astype(BF16))
        dgated = dgated_all[of[micro]]
        dgate = dgated * normed
        dnormed = dgated * gate
        dpre_ref[of[micro], :width] = (dgate * slope_ref[of[micro], :width].astype(F32)).astype(BF16)
        shared = jnp.mean(dnormed * normed, axis=1, keepdims=True)
        dcentred = inverse * (dnormed - normed * shared)
        datt = dcentred - jnp.mean(dcentred, axis=1, keepdims=True)
        datt_ref[of[micro], :] = datt.astype(BF16)
    mixed = mm(jnp.concatenate(gated_all, axis=0), w_out_ref[...])
    out_ref[...] = (emb_ref[...].astype(F32) + mixed).astype(BF16).reshape(out_ref.shape)
    send(out_ref, out_hbm)

    for micro in range(MB):
        for pair in range(pairs):
            first = 128 * pair
            at_value = slice(width + first, width + first + 128)
            at_query = slice(2 * width + first, 2 * width + first + 128)
            at_key = slice(3 * width + first, 3 * width + first + 128)
            value = hidden_ref[of[micro], at_value]
            query = hidden_ref[of[micro], at_query]
            key = hidden_ref[of[micro], at_key]
            dhead = datt_ref[of[micro], first : first + 128]
            dweights = mm_nt(both_heads(dhead, masks), value)
            parts = []
            for head in range(2):
                at = slice(length * head, length * head + length)
                parts.append((dweights[at] * dsilu_ref[micro * pairs + pair, :, at].astype(F32)).astype(BF16))
            dscore = jnp.concatenate(parts, axis=1)
            dquery = mm(dscore, both_heads(key, score_masks))
            dkeys = mm_tn(dscore, query * jnp.asarray(0.0625, BF16))
            dkey = jnp.where(lane < 64, dkeys[:length], dkeys[length:])
            dvalues = mm_tn(weight_ref[micro * pairs + pair], dhead)
            dvalue = jnp.where(lane < 64, dvalues[:length], dvalues[length:])
            for at, grad in ((at_value, dvalue), (at_query, dquery), (at_key, dkey)):
                dpre_ref[of[micro], at] = (grad * slope_ref[of[micro], at].astype(F32)).astype(BF16)

    grad_ref[...] = (cot.astype(F32) + mm_nt(dpre_ref[...], w_in_ref[...])).astype(BF16)
    groups, half, columns = sent_ref.shape

    theirs = pl.ds(pl.multiple_of((1 - half_ref[0]) * half, half), half)
    mine = pl.ds(pl.multiple_of(half_ref[0] * half, half), half)

    def weights(left_ref, right, first):
        left = jnp.concatenate([left_ref[theirs, :], left_ref[mine, :]], axis=0)
        part = mm(left, right).astype(BF16)
        start = first
        while start < first + right.shape[1]:
            group, inside = start // columns, start % columns
            count = min(columns - inside, first + right.shape[1] - start)
            here = part[:, start - first : start - first + count]
            sent_ref[group, :, inside : inside + count] = here[:half]
            kept_ref[group * half : (group + 1) * half, inside : inside + count] = here[half:]
            start += count

    for first in range(0, width4, 512):
        weights(emb_t_ref, dpre_ref[:, first : first + 512], first)
    weights(gated_t_ref, cot, width4)
    send(sent_ref, sent_hbm)
    places = iota((slots, length), 0)

    def placing(micro, shift):
        return jnp.where(places == flat_ref[micro : micro + 1, :] + shift, 1.0, 0.0).astype(BF16)

    pair = jnp.concatenate([placing(0, 0), placing(1, 4)], axis=1)
    back_ref[:, :width] = mm(pair, grad_ref[: 2 * length]).astype(BF16)
    last = jnp.concatenate([placing(2, 0), placing(2, 4)], axis=1)
    halves = [grad_ref[2 * length :, : width // 2], grad_ref[2 * length :, width // 2 :]]
    back_ref[:, width:] = mm(last, jnp.concatenate(halves, axis=0)).astype(BF16)
    send(back_ref, back_hbm)
    for copy in outgoing:
        copy.wait()


def layers(core, lengths, flat, rows, w_in, w_out, cotangent):
    width = w_in.shape[0]
    length = cotangent.shape[1]
    slots = rows.shape[0]
    columns = 5 * width // 4
    sent = (4, width // 2, columns)
    return pl.pallas_call(
        layers_kernel,
        out_shape=[
            jax.ShapeDtypeStruct(shape, BF16) for shape in [cotangent.shape, sent, rows.shape, (slots, columns)]
        ],
        in_specs=[SMEM, SMEM, VMEM, VMEM] + [HBM] * 3,
        out_specs=[HBM, HBM, HBM, VMEM],
        scratch_shapes=[
            pltpu.VMEM(shape, BF16)
            for shape in [
                w_in.shape,
                w_out.shape,
                cotangent.shape,
                cotangent.shape,
                (width, MB * length),
                (width, MB * length),
                (MB * length, 4 * width),
                (MB * length, width),
                sent,
                rows.shape,
                (MB * length, width),
                (MB * length, 4 * width),
                (MB * length, 4 * width),
                (MB * HEADS // 2, length, 2 * length),
                (MB * HEADS // 2, length, 2 * length),
            ]
        ]
        + [
            pltpu.VMEM((MB * length, width), F32),
            pltpu.VMEM((MB * length, width), BF16),
            pltpu.SemaphoreType.DMA((10,)),
            pltpu.SemaphoreType.DMA((3,)),
        ],
        compiler_params=params(46),
        cost_estimate=cost(28_000_000_000, 10 * 1024 * 1024),
        name="layers",
    )(core, lengths, flat, rows, w_in, w_out, cotangent)


def message_kernel(back_hbm, kept_ref, other_ref, out_ref, sem):
    skip = back_hbm.shape[1]
    copy = pltpu.make_async_copy(back_hbm, out_ref.at[:, pl.ds(0, skip)], sem)
    copy.start()
    out_ref[:, skip:] = (kept_ref[...].astype(F32) + other_ref[...].astype(F32)).astype(BF16)
    copy.wait()


def message(back, kept, other):
    return pl.pallas_call(
        message_kernel,
        out_shape=jax.ShapeDtypeStruct((back.shape[0], back.shape[1] + kept.shape[1]), BF16),
        in_specs=[HBM, VMEM, VMEM],
        out_specs=VMEM,
        scratch_shapes=[pltpu.SemaphoreType.DMA],
        compiler_params=params(16),
        cost_estimate=cost(1_000_000, 4 * 1024 * 1024),
        name="message",
    )(back, kept, other)


def shard_sum_kernel(in_ref, out_ref, *, skip, factor):
    slots = in_ref.shape[0]
    parts = in_ref[:, skip:].astype(F32).reshape(slots // 16, 16, in_ref.shape[1] - skip)
    summed = (jnp.sum(parts, axis=0) * factor).astype(BF16)
    out_ref[...] = jnp.broadcast_to(summed[None], (slots // 16, *summed.shape)).reshape(out_ref.shape)


def shard_sum(arrived, skip, factor):
    slots = arrived.shape[0]
    return pl.pallas_call(
        functools.partial(shard_sum_kernel, skip=skip, factor=factor),
        out_shape=jax.ShapeDtypeStruct((slots, arrived.shape[1] - skip), BF16),
        in_specs=[VMEM],
        out_specs=VMEM,
        compiler_params=params(16),
        cost_estimate=cost(1_000_000, 4 * 1024 * 1024),
        name="shard_sum",
    )(arrived)


def table_grad_kernel(pair_row_ref, last_row_ref, arrived_ref, out_ref, last_rows_ref):
    step = pl.program_id(0)
    block, width = out_ref.shape

    @pl.when(step == 0)
    def _():
        last_rows_ref[...] = unfold(arrived_ref[:, width : width + width // 2].astype(F32)).astype(BF16)

    def hot(row):
        places = iota((block, row.shape[1]), 0)
        return jnp.where(places == row - step * block, 1.0, 0.0).astype(BF16)

    out_ref[...] = mm(hot(pair_row_ref[...]), arrived_ref[:, :width]) + mm(
        hot(last_row_ref[...]), last_rows_ref[...]
    )


def table_gradient(pair_row, last_row, arrived, own_rows, width):
    steps = 8
    block = own_rows // steps

    def whole(shape):
        return pl.BlockSpec(shape, lambda i: (0,) * len(shape))

    return pl.pallas_call(
        table_grad_kernel,
        out_shape=jax.ShapeDtypeStruct((own_rows, width), F32),
        grid=(steps,),
        in_specs=[whole(pair_row.shape), whole(last_row.shape), whole(arrived.shape)],
        out_specs=pl.BlockSpec((block, width), lambda i: (i, 0)),
        scratch_shapes=[pltpu.VMEM((last_row.shape[1], width), BF16)],
        compiler_params=params(24),
        cost_estimate=cost(2 * own_rows * 1536 * width, 12 * 1024 * 1024),
        name="table_grad",
    )(pair_row, last_row, arrived)


def finish_kernel(half_ref, in_ref, *rest):
    del half_ref
    win_ref, wout_ref = rest[-2:]
    groups, _, columns = in_ref.shape
    width4 = win_ref.shape[1]
    for group in range(groups):
        first = group * columns
        last = min(first + columns, width4)
        win_ref[:, first:last] = in_ref[group, :, : last - first].astype(F32)
    wout_ref[...] = in_ref[groups - 1, :, width4 - (groups - 1) * columns :].astype(F32)


def finish(half_index, part, before, width, width4):
    half = width // 2
    shape = part.shape
    steps = 2
    return pl.pallas_call(
        finish_kernel,
        out_shape=(jax.ShapeDtypeStruct((width, width4), F32), jax.ShapeDtypeStruct((width, width), F32)),
        grid_spec=pltpu.PrefetchScalarGridSpec(
            num_scalar_prefetch=1,
            grid=(steps,),
            in_specs=[pl.BlockSpec((shape[0], shape[1] // steps, shape[2]), lambda i, which: (0, i, 0))]
            + [pl.BlockSpec(memory_space=pl.ANY)] * len(before),
            out_specs=(
                pl.BlockSpec((half // steps, width4), lambda i, which: (which[0] * steps + i, 0)),
                pl.BlockSpec((half // steps, width), lambda i, which: (which[0] * steps + i, 0)),
            ),
        ),
        input_output_aliases={2: 0, 3: 1} if before else {},
        compiler_params=params(16),
        cost_estimate=cost(1_000_000, 4 * 1024 * 1024),
        name=f"finish{len(before)}",
    )(half_index, part, *before)


def trade(payload):
    return lax.all_to_all(payload, AXES, split_axis=0, concat_axis=0, tiled=True)


def shards(table, w_in, w_out, item_owner, item_slot, seq_lengths, cotangent):
    table_axis = lax.axis_size("table")
    owners_n = lax.axis_size("dp") * table_axis
    length = item_slot.shape[1]
    own_rows, width = table.shape
    slots = owners_n * 8
    core = (lax.axis_index("table") % 2).astype(I32).reshape(1)
    swap = [(i, i ^ 1) for i in range(table_axis)]

    wanted, flat = requests(item_owner.reshape(MB, 1, length), item_slot, owners_n)
    asked = trade(wanted)
    rows = trade(gather(asked, table))
    pair_row = asked[:, :8].reshape(1, slots)
    last_row = asked[:, 8:12].reshape(1, slots // 2)
    out, sent, back, kept = layers(core, seq_lengths, flat, rows, w_in, w_out, cotangent)
    columns = sent.shape[2]
    other = lax.ppermute(sent.reshape(slots, columns), "table", swap)
    arrived = trade(message(back, kept, other))
    factor = (MB * length * owners_n) ** (-0.5)
    mine_full = trade(shard_sum(arrived, rows.shape[1], factor))
    table_grad = table_gradient(pair_row, last_row, arrived, own_rows, width)
    mine_full, table_grad = lax.optimization_barrier((mine_full, table_grad))
    other_full = lax.ppermute(mine_full, "table", swap)
    shape = (4, width // 2, columns)
    partial = finish(core, mine_full.reshape(shape), (), width, w_in.shape[1])
    win_grad, wout_grad = finish(1 - core, other_full.reshape(shape), partial, width, w_in.shape[1])
    return out, table_grad, win_grad, wout_grad


def solution(mesh):
    in_specs = (
        P(AXES, None),
        P(),
        P(),
        P(None, AXES, None),
        P(None, AXES),
        P(None, AXES, None),
        P(None, AXES, None),
    )
    out_specs = (P(None, AXES, None), P(AXES, None), P(), P())
    return jax.shard_map(shards, mesh=mesh, in_specs=in_specs, out_specs=out_specs, check_vma=False)
```

```python
import functools

import jax
import jax.numpy as jnp
from jax import lax
from jax.experimental import pallas as pl
from jax.experimental.pallas import tpu as pltpu
from jax.sharding import Mesh
from jax.sharding import PartitionSpec as P

HEADS = 8
MB = 3
CAP = 4
AXES = ("dp", "y", "core")
F32 = jnp.float32
BF16 = jnp.bfloat16
I32 = jnp.int32
VMEM = pl.BlockSpec(memory_space=pltpu.VMEM)
HBM = pl.BlockSpec(memory_space=pltpu.HBM)
SMEM = pl.BlockSpec(memory_space=pltpu.SMEM)


def iota(shape, dim):
    return lax.broadcasted_iota(I32, shape, dim)


def mm(a, b):
    return jnp.dot(a, b, preferred_element_type=F32)


def mm_nt(a, b):
    return lax.dot_general(a, b, (((1,), (1,)), ((), ())), preferred_element_type=F32)


def mm_tn(a, b):
    return lax.dot_general(a, b, (((0,), (0,)), ((), ())), preferred_element_type=F32)


def params(mib):
    return pltpu.CompilerParams(vmem_limit_bytes=mib * 1024 * 1024)


def cost(flops, bytes_accessed):
    return pl.CostEstimate(flops=flops, bytes_accessed=bytes_accessed, transcendentals=0)


def request_kernel(owner_ref, slot_ref, wanted_ref, flat_ref):
    length = slot_ref.shape[1]
    owners_n = wanted_ref.shape[0]
    upto = (iota((length, length), 0) <= iota((length, length), 1)).astype(BF16)
    lane_row = iota((128, length), 0)
    high = jnp.zeros((owners_n, 128), F32)
    low = jnp.zeros((owners_n, 128), F32)
    live = jnp.zeros((owners_n, 128), F32)
    flat_ref[...] = jnp.zeros(flat_ref.shape, I32)
    for micro in range(MB):
        owner = owner_ref[micro]
        slot = slot_ref[micro : micro + 1, :]
        hot = (iota((owners_n, length), 0) == owner).astype(F32)
        hot_bf = hot.astype(BF16)
        counts = mm(hot_bf, upto)
        rank = (jnp.sum(counts * hot, axis=0, keepdims=True) - 1.0).astype(I32)
        flat_ref[micro : micro + 1, :] = owner * 8 + rank
        here = lane_row == rank + CAP * micro
        high = high + mm_nt(hot_bf, jnp.where(here, (slot >> 6).astype(F32), 0.0).astype(BF16))
        low = low + mm_nt(hot_bf, jnp.where(here, (slot & 63).astype(F32), 0.0).astype(BF16))
        live = live + mm_nt(hot_bf, jnp.where(here, 1.0, 0.0).astype(BF16))
    wanted_ref[...] = jnp.where(live > 0.5, high * 64.0 + low, -1.0).astype(I32)


def requests(owner, slot, owners_n):
    return pl.pallas_call(
        request_kernel,
        out_shape=(
            jax.ShapeDtypeStruct((owners_n, 128), I32),
            jax.ShapeDtypeStruct((8, slot.shape[1]), I32),
        ),
        grid=(1,),
        in_specs=[
            pl.BlockSpec(owner.shape, lambda i: (0, 0, 0)),
            pl.BlockSpec(slot.shape, lambda i: (0, 0)),
        ],
        out_specs=(
            pl.BlockSpec((owners_n, 128), lambda i: (0, 0)),
            pl.BlockSpec((8, slot.shape[1]), lambda i: (0, 0)),
        ),
        compiler_params=params(8),
        name="requests",
    )(owner, slot)


def unfold(folded):
    half = folded.shape[1]
    whole = folded.reshape(folded.shape[0] // 16, 16, half)
    even, odd = whole[:, :8], whole[:, 8:]
    top = iota(even.shape, 1) < 4
    left = jnp.where(top, even, pltpu.roll(odd, 4, 1))
    right = jnp.where(top, pltpu.roll(even, 4, 1), odd)
    return jnp.concatenate([left, right], axis=2).reshape(folded.shape[0] // 2, 2 * half)


def gather_kernel(asked_hbm, table_hbm, out_ref, asked_ref, block_ref, wide_ref, sem):
    steps, block, columns = block_ref.shape
    devices = asked_ref.shape[0]
    copies = [pltpu.make_async_copy(asked_hbm, asked_ref, sem.at[steps])]
    for step in range(steps):
        source = table_hbm.at[pl.ds(step * block, block)]
        copies.append(pltpu.make_async_copy(source, block_ref.at[step], sem.at[step]))
    for copy in copies:
        copy.start()
    for step in range(steps):
        copies[1 + step].wait()
        wide_ref[step * block : (step + 1) * block, :] = block_ref[step].astype(F32)
    copies[0].wait()
    half = columns // 2
    below = iota((8, columns), 0)
    below_half = iota((8, half), 0)

    def two_devices(turn, carry):
        pairs = []
        lasts = []
        for which in range(2):
            names = [jnp.maximum(asked_ref[2 * turn + which, place], 0) for place in range(12)]
            rows = [wide_ref[pl.ds(name, 1), :] for name in names]
            tile = jnp.broadcast_to(rows[0], (8, columns))
            for place in range(1, 8):
                tile = jnp.where(below == place, rows[place], tile)
            pairs.append(tile)
            parts = [row[:, :half] for row in rows[8:]] + [row[:, half:] for row in rows[8:]]
            tile = jnp.broadcast_to(parts[0], (8, half))
            for place in range(1, 8):
                tile = jnp.where(below_half == place, parts[place], tile)
            lasts.append(tile)
        at = pl.ds(pl.multiple_of(16 * turn, 16), 16)
        out_ref[at, :columns] = jnp.concatenate(pairs, axis=0).astype(BF16)
        out_ref[at, columns:] = jnp.concatenate(lasts, axis=0).astype(BF16)
        return carry

    lax.fori_loop(0, devices // 2, two_devices, 0)


def gather(asked, table):
    own_rows, columns = table.shape
    devices = asked.shape[0]
    steps = 8
    return pl.pallas_call(
        gather_kernel,
        out_shape=jax.ShapeDtypeStruct((devices * 8, columns + columns // 2), BF16),
        in_specs=[HBM, HBM],
        out_specs=VMEM,
        scratch_shapes=[
            pltpu.SMEM(asked.shape, I32),
            pltpu.VMEM((steps, own_rows // steps, columns), BF16),
            pltpu.VMEM((own_rows, columns), F32),
            pltpu.SemaphoreType.DMA((steps + 1,)),
        ],
        compiler_params=params(59),
        cost_estimate=cost(6_000_000_000, 6 * 1024 * 1024),
        name="gather",
    )(asked, table)


def column_of(row, copies=128):
    return jnp.transpose(jnp.broadcast_to(row.astype(F32), (copies, row.shape[1])))


def both_heads(pair_columns, masks):
    return jnp.concatenate([pair_columns * masks[0], pair_columns * masks[1]], axis=0)


def layers_kernel(half_ref, lengths_ref, flat_ref, rows_ref, w_in_hbm, w_out_hbm, cot_hbm, *rest):
    out_hbm, sent_hbm, back_hbm, kept_ref = rest[:4]
    w_in_ref, w_out_ref, cot_ref, out_ref, emb_t_ref, gated_t_ref, dpre_ref, grad_ref, sent_ref, back_ref = rest[4:14]
    emb_ref, hidden_ref, slope_ref, weight_ref, dsilu_ref, att_ref, datt_ref, in_sem, out_sem = rest[14:]
    slots = rows_ref.shape[0]
    width = w_out_ref.shape[0]
    length = cot_hbm.shape[1]
    width4 = w_in_ref.shape[1]
    chunk = 512
    chunks = [slice(first, first + chunk) for first in range(0, width4, chunk)]
    incoming = []

    def bring(source, target):
        incoming.append(pltpu.make_async_copy(source, target, in_sem.at[len(incoming)]))
        incoming[-1].start()

    for part in chunks:
        at = pl.ds(part.start, chunk)
        bring(w_in_hbm.at[:, at], w_in_ref.at[:, at])
    bring(w_out_hbm, w_out_ref)
    bring(cot_hbm, cot_ref)
    outgoing = []

    def send(source, target):
        outgoing.append(pltpu.make_async_copy(source, target, out_sem.at[len(outgoing)]))
        outgoing[-1].start()

    of = [slice(micro * length, (micro + 1) * length) for micro in range(MB)]
    for micro in range(MB):
        column = column_of(flat_ref[micro : micro + 1, :])

        def placed(shift, column=column):
            lanes = iota((length, 128), 1).astype(F32)
            parts = [
                jnp.where(column == lanes + float(first - shift), 1.0, 0.0).astype(BF16)
                for first in range(0, slots, 128)
            ]
            return jnp.concatenate(parts, axis=1)

        if micro == 2:
            rows = rows_ref[:, width:]
            embedded = jnp.concatenate([mm(placed(0), rows), mm(placed(4), rows)], axis=1)
        else:
            embedded = mm(placed(4 * micro), rows_ref[:, :width])
        emb_ref[of[micro], :] = embedded.astype(BF16)
        emb_t_ref[:, of[micro]] = jnp.transpose(embedded).astype(BF16)

    for which, at in enumerate(chunks):
        incoming[which].wait()
        half = mm(emb_ref[...], w_in_ref[:, at]) * 0.5
        tanh = jnp.tanh(half)
        act = half + half * tanh
        hidden_ref[:, at] = act.astype(BF16)
        slope_ref[:, at] = (0.5 * ((1.0 + tanh) + act * (1.0 - tanh))).astype(BF16)

    lane = iota((1, 128), 1)
    first_head = (lane < 64).astype(F32)
    second_head = 1.0 - first_head
    masks = (first_head.astype(BF16), second_head.astype(BF16))
    score_masks = ((first_head * 0.0625).astype(BF16), (second_head * 0.0625).astype(BF16))
    pairs = HEADS // 2
    query_at = iota((length, length), 0)
    key_at = iota((length, length), 1)
    for micro in range(MB):
        ends = []
        total = 0
        for which in range(3):
            total = total + lengths_ref[micro, 0, which]
            ends.append(total)

        def segment(places, ends=ends):
            return sum((places >= end).astype(I32) for end in ends)

        allowed = (segment(query_at) == segment(key_at)) & (key_at <= query_at)
        for pair in range(pairs):
            first = 128 * pair
            value = hidden_ref[of[micro], width + first : width + first + 128]
            query = hidden_ref[of[micro], 2 * width + first : 2 * width + first + 128]
            key = hidden_ref[of[micro], 3 * width + first : 3 * width + first + 128]
            halves = mm_nt(both_heads(query, score_masks), key)
            for head in range(2):
                at = slice(length * head, length * head + length)
                half = halves[at]
                tanh = jnp.tanh(half)
                act = half + half * tanh
                weight_ref[micro * pairs + pair, :, at] = jnp.where(allowed, act, 0.0).astype(BF16)
                dsilu_ref[micro * pairs + pair, :, at] = jnp.where(
                    allowed, (1.0 + tanh) + act * (1.0 - tanh), 0.0
                ).astype(BF16)
            att_ref[of[micro], first : first + 128] = mm(
                weight_ref[micro * pairs + pair], both_heads(value, masks)
            )

    incoming[-2].wait()
    incoming[-1].wait()
    cot = cot_ref[...].reshape(MB * length, width)
    dgated_all = mm_nt(cot, w_out_ref[...])
    gated_all = []
    for micro in range(MB):
        attended = att_ref[of[micro], :]
        centred = attended - jnp.mean(attended, axis=1, keepdims=True)
        inverse = lax.rsqrt(jnp.mean(centred * centred, axis=1, keepdims=True) + 1e-05)
        normed = centred * inverse
        gate = hidden_ref[of[micro], :width].astype(F32)
        gated = normed * gate
        gated_t_ref[:, of[micro]] = jnp.transpose(gated).astype(BF16)
        gated_all.append(gated.astype(BF16))
        dgated = dgated_all[of[micro]]
        dgate = dgated * normed
        dnormed = dgated * gate
        dpre_ref[of[micro], :width] = (dgate * slope_ref[of[micro], :width].astype(F32)).astype(BF16)
        shared = jnp.mean(dnormed * normed, axis=1, keepdims=True)
        dcentred = inverse * (dnormed - normed * shared)
        datt = dcentred - jnp.mean(dcentred, axis=1, keepdims=True)
        datt_ref[of[micro], :] = datt.astype(BF16)
    mixed = mm(jnp.concatenate(gated_all, axis=0), w_out_ref[...])
    out_ref[...] = (emb_ref[...].astype(F32) + mixed).astype(BF16).reshape(out_ref.shape)
    send(out_ref, out_hbm)

    for micro in range(MB):
        for pair in range(pairs):
            first = 128 * pair
            at_value = slice(width + first, width + first + 128)
            at_query = slice(2 * width + first, 2 * width + first + 128)
            at_key = slice(3 * width + first, 3 * width + first + 128)
            value = hidden_ref[of[micro], at_value]
            query = hidden_ref[of[micro], at_query]
            key = hidden_ref[of[micro], at_key]
            dhead = datt_ref[of[micro], first : first + 128]
            dweights = mm_nt(both_heads(dhead, masks), value)
            parts = []
            for head in range(2):
                at = slice(length * head, length * head + length)
                parts.append((dweights[at] * dsilu_ref[micro * pairs + pair, :, at].astype(F32)).astype(BF16))
            dscore = jnp.concatenate(parts, axis=1)
            dquery = mm(dscore, both_heads(key, score_masks))
            dkeys = mm_tn(dscore, query * jnp.asarray(0.0625, BF16))
            dkey = jnp.where(lane < 64, dkeys[:length], dkeys[length:])
            dvalues = mm_tn(weight_ref[micro * pairs + pair], dhead)
            dvalue = jnp.where(lane < 64, dvalues[:length], dvalues[length:])
            for at, grad in ((at_value, dvalue), (at_query, dquery), (at_key, dkey)):
                dpre_ref[of[micro], at] = (grad * slope_ref[of[micro], at].astype(F32)).astype(BF16)

    grad_ref[...] = (cot.astype(F32) + mm_nt(dpre_ref[...], w_in_ref[...])).astype(BF16)
    groups, half, columns = sent_ref.shape

    theirs = pl.ds(pl.multiple_of((1 - half_ref[0]) * half, half), half)
    mine = pl.ds(pl.multiple_of(half_ref[0] * half, half), half)

    def weights(left_ref, right, first):
        left = jnp.concatenate([left_ref[theirs, :], left_ref[mine, :]], axis=0)
        part = mm(left, right).astype(BF16)
        start = first
        while start < first + right.shape[1]:
            group, inside = start // columns, start % columns
            count = min(columns - inside, first + right.shape[1] - start)
            here = part[:, start - first : start - first + count]
            sent_ref[group, :, inside : inside + count] = here[:half]
            kept_ref[group * half : (group + 1) * half, inside : inside + count] = here[half:]
            start += count

    for first in range(0, width4, 512):
        weights(emb_t_ref, dpre_ref[:, first : first + 512], first)
    weights(gated_t_ref, cot, width4)
    send(sent_ref, sent_hbm)
    places = iota((slots, length), 0)

    def placing(micro, shift):
        return jnp.where(places == flat_ref[micro : micro + 1, :] + shift, 1.0, 0.0).astype(BF16)

    pair = jnp.concatenate([placing(0, 0), placing(1, 4)], axis=1)
    back_ref[:, :width] = mm(pair, grad_ref[: 2 * length]).astype(BF16)
    last = jnp.concatenate([placing(2, 0), placing(2, 4)], axis=1)
    halves = [grad_ref[2 * length :, : width // 2], grad_ref[2 * length :, width // 2 :]]
    back_ref[:, width:] = mm(last, jnp.concatenate(halves, axis=0)).astype(BF16)
    send(back_ref, back_hbm)
    for copy in outgoing:
        copy.wait()


def layers(core, lengths, flat, rows, w_in, w_out, cotangent):
    width = w_in.shape[0]
    length = cotangent.shape[1]
    slots = rows.shape[0]
    columns = 5 * width // 4
    sent = (4, width // 2, columns)
    return pl.pallas_call(
        layers_kernel,
        out_shape=[
            jax.ShapeDtypeStruct(shape, BF16) for shape in [cotangent.shape, sent, rows.shape, (slots, columns)]
        ],
        in_specs=[SMEM, SMEM, VMEM, VMEM] + [HBM] * 3,
        out_specs=[HBM, HBM, HBM, VMEM],
        scratch_shapes=[
            pltpu.VMEM(shape, BF16)
            for shape in [
                w_in.shape,
                w_out.shape,
                cotangent.shape,
                cotangent.shape,
                (width, MB * length),
                (width, MB * length),
                (MB * length, 4 * width),
                (MB * length, width),
                sent,
                rows.shape,
                (MB * length, width),
                (MB * length, 4 * width),
                (MB * length, 4 * width),
                (MB * HEADS // 2, length, 2 * length),
                (MB * HEADS // 2, length, 2 * length),
            ]
        ]
        + [
            pltpu.VMEM((MB * length, width), F32),
            pltpu.VMEM((MB * length, width), BF16),
            pltpu.SemaphoreType.DMA((10,)),
            pltpu.SemaphoreType.DMA((3,)),
        ],
        compiler_params=params(46),
        cost_estimate=cost(28_000_000_000, 10 * 1024 * 1024),
        name="layers",
    )(core, lengths, flat, rows, w_in, w_out, cotangent)


def message_kernel(back_hbm, kept_ref, other_ref, out_ref, sem):
    skip = back_hbm.shape[1]
    copy = pltpu.make_async_copy(back_hbm, out_ref.at[:, pl.ds(0, skip)], sem)
    copy.start()
    out_ref[:, skip:] = (kept_ref[...].astype(F32) + other_ref[...].astype(F32)).astype(BF16)
    copy.wait()


def message(back, kept, other):
    return pl.pallas_call(
        message_kernel,
        out_shape=jax.ShapeDtypeStruct((back.shape[0], back.shape[1] + kept.shape[1]), BF16),
        in_specs=[HBM, VMEM, VMEM],
        out_specs=VMEM,
        scratch_shapes=[pltpu.SemaphoreType.DMA],
        compiler_params=params(16),
        cost_estimate=cost(1_000_000, 4 * 1024 * 1024),
        name="message",
    )(back, kept, other)


def shard_sum_kernel(in_ref, out_ref, *, skip, factor):
    slots = in_ref.shape[0]
    parts = in_ref[:, skip:].astype(F32).reshape(slots // 16, 16, in_ref.shape[1] - skip)
    summed = (jnp.sum(parts, axis=0) * factor).astype(BF16)
    out_ref[...] = jnp.broadcast_to(summed[None], (slots // 16, *summed.shape)).reshape(out_ref.shape)


def shard_sum(arrived, skip, factor):
    slots = arrived.shape[0]
    return pl.pallas_call(
        functools.partial(shard_sum_kernel, skip=skip, factor=factor),
        out_shape=jax.ShapeDtypeStruct((slots, arrived.shape[1] - skip), BF16),
        in_specs=[VMEM],
        out_specs=VMEM,
        compiler_params=params(16),
        cost_estimate=cost(1_000_000, 4 * 1024 * 1024),
        name="shard_sum",
    )(arrived)


def table_grad_kernel(pair_row_ref, last_row_ref, arrived_ref, out_ref, last_rows_ref):
    step = pl.program_id(0)
    block, width = out_ref.shape

    @pl.when(step == 0)
    def _():
        last_rows_ref[...] = unfold(arrived_ref[:, width : width + width // 2].astype(F32)).astype(BF16)

    def hot(row):
        places = iota((block, row.shape[1]), 0)
        return jnp.where(places == row - step * block, 1.0, 0.0).astype(BF16)

    out_ref[...] = mm(hot(pair_row_ref[...]), arrived_ref[:, :width]) + mm(
        hot(last_row_ref[...]), last_rows_ref[...]
    )


def table_gradient(pair_row, last_row, arrived, own_rows, width):
    steps = 8
    block = own_rows // steps

    def whole(shape):
        return pl.BlockSpec(shape, lambda i: (0,) * len(shape))

    return pl.pallas_call(
        table_grad_kernel,
        out_shape=jax.ShapeDtypeStruct((own_rows, width), F32),
        grid=(steps,),
        in_specs=[whole(pair_row.shape), whole(last_row.shape), whole(arrived.shape)],
        out_specs=pl.BlockSpec((block, width), lambda i: (i, 0)),
        scratch_shapes=[pltpu.VMEM((last_row.shape[1], width), BF16)],
        compiler_params=params(24),
        cost_estimate=cost(2 * own_rows * 1536 * width, 12 * 1024 * 1024),
        name="table_grad",
    )(pair_row, last_row, arrived)


def finish_kernel(core_ref, in_ref, *rest):
    del core_ref
    win_ref, wout_ref = rest[-2:]
    groups, _, _, columns = in_ref.shape
    width4 = win_ref.shape[-1]
    for group in range(groups):
        first = group * columns
        last = min(first + columns, width4)
        part = in_ref[group].astype(F32)
        for half in range(2):
            rows = part[:, 8 * half : 8 * half + 8]
            win_ref[half, :, 0, :, first:last] = rows[:, :, : last - first]
            if group == groups - 1:
                wout_ref[half, :, 0] = rows[:, :, last - first :]


def finish(core, part, before, width, width4):
    across = width // 32
    part = part.reshape(4, across, 16, part.shape[1])
    steps = 2
    block = across // steps
    shapes = [(2, across, 2, 8, width4), (2, across, 2, 8, width)]
    return pl.pallas_call(
        finish_kernel,
        out_shape=[jax.ShapeDtypeStruct(shape, F32) for shape in shapes],
        grid_spec=pltpu.PrefetchScalarGridSpec(
            num_scalar_prefetch=1,
            grid=(steps,),
            in_specs=[pl.BlockSpec((4, block, 16, part.shape[3]), lambda i, which: (0, i, 0, 0))]
            + [pl.BlockSpec(memory_space=pl.ANY)] * len(before),
            out_specs=[
                pl.BlockSpec((2, block, 1, 8, shape[4]), lambda i, which: (0, i, which[0], 0, 0)) for shape in shapes
            ],
        ),
        input_output_aliases={2: 0, 3: 1} if before else {},
        compiler_params=params(16),
        cost_estimate=cost(1_000_000, 4 * 1024 * 1024),
        name=f"finish{len(before)}",
    )(core, part, *before)


def trade(payload, axes=AXES):
    return lax.all_to_all(payload, axes, split_axis=0, concat_axis=0, tiled=True)


def shards(table, w_in, w_out, item_owner, item_slot, seq_lengths, cotangent):
    owners_n = lax.axis_size(AXES)
    length = item_slot.shape[1]
    own_rows, width = table.shape
    slots = owners_n * 8
    core = lax.axis_index("core").astype(I32).reshape(1)
    swap = [(0, 1), (1, 0)]

    wanted, flat = requests(item_owner.reshape(MB, 1, length), item_slot, owners_n)
    asked = trade(wanted)
    rows = trade(gather(asked, table))
    pair_row = asked[:, :8].reshape(1, slots)
    last_row = asked[:, 8:12].reshape(1, slots // 2)
    out, sent, back, kept = layers(core, seq_lengths, flat, rows, w_in, w_out, cotangent)
    columns = sent.shape[2]
    other = lax.ppermute(sent.reshape(slots, columns), "core", swap)
    arrived = trade(message(back, kept, other))
    factor = (MB * length * owners_n) ** (-0.5)
    mine_full = trade(shard_sum(arrived, rows.shape[1], factor), AXES[:2])
    table_grad = table_gradient(pair_row, last_row, arrived, own_rows, width)
    mine_full, table_grad = lax.optimization_barrier((mine_full, table_grad))
    other_full = lax.ppermute(mine_full, "core", swap)
    width4 = w_in.shape[1]
    partial = finish(core, mine_full, (), width, width4)
    win_grad, wout_grad = finish(1 - core, other_full, partial, width, width4)
    return out, table_grad, win_grad.reshape(width, width4), wout_grad.reshape(width, width)


def solution(mesh):
    dp, table_axis = mesh.devices.shape
    mesh = Mesh(mesh.devices.reshape(dp, table_axis // 2, 2), AXES)
    in_specs = (
        P(AXES, None),
        P(),
        P(),
        P(None, AXES, None),
        P(None, AXES),
        P(None, AXES, None),
        P(None, AXES, None),
    )
    out_specs = (P(None, AXES, None), P(AXES, None), P(), P())
    return jax.shard_map(shards, mesh=mesh, in_specs=in_specs, out_specs=out_specs, check_vma=False)
```

```python
import functools

import jax
import jax.numpy as jnp
from jax import lax
from jax.experimental import pallas as pl
from jax.experimental.pallas import tpu as pltpu
from jax.sharding import Mesh
from jax.sharding import PartitionSpec as P

HEADS = 8
MB = 3
CAP = 4
AXES = ("dp", "y", "core")
F32 = jnp.float32
BF16 = jnp.bfloat16
I32 = jnp.int32
VMEM = pl.BlockSpec(memory_space=pltpu.VMEM)
HBM = pl.BlockSpec(memory_space=pltpu.HBM)
SMEM = pl.BlockSpec(memory_space=pltpu.SMEM)


def iota(shape, dim):
    return lax.broadcasted_iota(I32, shape, dim)


def mm(a, b):
    return jnp.dot(a, b, preferred_element_type=F32)


def mm_nt(a, b):
    return lax.dot_general(a, b, (((1,), (1,)), ((), ())), preferred_element_type=F32)


def mm_tn(a, b):
    return lax.dot_general(a, b, (((0,), (0,)), ((), ())), preferred_element_type=F32)


def params(mib):
    return pltpu.CompilerParams(vmem_limit_bytes=mib * 1024 * 1024)


def cost(flops, bytes_accessed):
    return pl.CostEstimate(flops=flops, bytes_accessed=bytes_accessed, transcendentals=0)


def request_kernel(owner_ref, slot_ref, wanted_ref, flat_ref):
    length = slot_ref.shape[1]
    owners_n = wanted_ref.shape[0]
    upto = (iota((length, length), 0) <= iota((length, length), 1)).astype(BF16)
    lane_row = iota((128, length), 0)
    high = jnp.zeros((owners_n, 128), F32)
    low = jnp.zeros((owners_n, 128), F32)
    live = jnp.zeros((owners_n, 128), F32)
    flat_ref[...] = jnp.zeros(flat_ref.shape, I32)
    for micro in range(MB):
        owner = owner_ref[micro]
        slot = slot_ref[micro : micro + 1, :]
        hot = (iota((owners_n, length), 0) == owner).astype(F32)
        hot_bf = hot.astype(BF16)
        counts = mm(hot_bf, upto)
        rank = (jnp.sum(counts * hot, axis=0, keepdims=True) - 1.0).astype(I32)
        flat_ref[micro : micro + 1, :] = owner * 8 + rank
        here = lane_row == rank + CAP * micro
        high = high + mm_nt(hot_bf, jnp.where(here, (slot >> 6).astype(F32), 0.0).astype(BF16))
        low = low + mm_nt(hot_bf, jnp.where(here, (slot & 63).astype(F32), 0.0).astype(BF16))
        live = live + mm_nt(hot_bf, jnp.where(here, 1.0, 0.0).astype(BF16))
    wanted_ref[...] = jnp.where(live > 0.5, high * 64.0 + low, -1.0).astype(I32)


def requests(owner, slot, owners_n):
    return pl.pallas_call(
        request_kernel,
        out_shape=(
            jax.ShapeDtypeStruct((owners_n, 128), I32),
            jax.ShapeDtypeStruct((8, slot.shape[1]), I32),
        ),
        grid=(1,),
        in_specs=[
            pl.BlockSpec(owner.shape, lambda i: (0, 0, 0)),
            pl.BlockSpec(slot.shape, lambda i: (0, 0)),
        ],
        out_specs=(
            pl.BlockSpec((owners_n, 128), lambda i: (0, 0)),
            pl.BlockSpec((8, slot.shape[1]), lambda i: (0, 0)),
        ),
        compiler_params=params(8),
        name="requests",
    )(owner, slot)


def unfold(folded):
    half = folded.shape[1]
    whole = folded.reshape(folded.shape[0] // 16, 16, half)
    even, odd = whole[:, :8], whole[:, 8:]
    top = iota(even.shape, 1) < 4
    left = jnp.where(top, even, pltpu.roll(odd, 4, 1))
    right = jnp.where(top, pltpu.roll(even, 4, 1), odd)
    return jnp.concatenate([left, right], axis=2).reshape(folded.shape[0] // 2, 2 * half)


def gather_kernel(asked_hbm, table_hbm, out_ref, asked_ref, block_ref, wide_ref, sem):
    steps, block, columns = block_ref.shape
    devices = asked_ref.shape[0]
    copies = [pltpu.make_async_copy(asked_hbm, asked_ref, sem.at[steps])]
    for step in range(steps):
        source = table_hbm.at[pl.ds(step * block, block)]
        copies.append(pltpu.make_async_copy(source, block_ref.at[step], sem.at[step]))
    for copy in copies:
        copy.start()
    for step in range(steps):
        copies[1 + step].wait()
        wide_ref[step * block : (step + 1) * block, :] = block_ref[step].astype(F32)
    copies[0].wait()
    half = columns // 2
    below = iota((8, columns), 0)
    below_half = iota((8, half), 0)

    def two_devices(turn, carry):
        pairs = []
        lasts = []
        for which in range(2):
            names = [jnp.maximum(asked_ref[2 * turn + which, place], 0) for place in range(12)]
            rows = [wide_ref[pl.ds(name, 1), :] for name in names]
            tile = jnp.broadcast_to(rows[0], (8, columns))
            for place in range(1, 8):
                tile = jnp.where(below == place, rows[place], tile)
            pairs.append(tile)
            parts = [row[:, :half] for row in rows[8:]] + [row[:, half:] for row in rows[8:]]
            tile = jnp.broadcast_to(parts[0], (8, half))
            for place in range(1, 8):
                tile = jnp.where(below_half == place, parts[place], tile)
            lasts.append(tile)
        at = pl.ds(pl.multiple_of(16 * turn, 16), 16)
        out_ref[at, :columns] = jnp.concatenate(pairs, axis=0).astype(BF16)
        out_ref[at, columns:] = jnp.concatenate(lasts, axis=0).astype(BF16)
        return carry

    lax.fori_loop(0, devices // 2, two_devices, 0)


def gather(asked, table):
    own_rows, columns = table.shape
    devices = asked.shape[0]
    steps = 8
    return pl.pallas_call(
        gather_kernel,
        out_shape=jax.ShapeDtypeStruct((devices * 8, columns + columns // 2), BF16),
        in_specs=[HBM, HBM],
        out_specs=VMEM,
        scratch_shapes=[
            pltpu.SMEM(asked.shape, I32),
            pltpu.VMEM((steps, own_rows // steps, columns), BF16),
            pltpu.VMEM((own_rows, columns), F32),
            pltpu.SemaphoreType.DMA((steps + 1,)),
        ],
        compiler_params=params(59),
        cost_estimate=cost(6_000_000_000, 6 * 1024 * 1024),
        name="gather",
    )(asked, table)


def column_of(row, copies=128):
    return jnp.transpose(jnp.broadcast_to(row.astype(F32), (copies, row.shape[1])))


def both_heads(pair_columns, masks):
    return jnp.concatenate([pair_columns * masks[0], pair_columns * masks[1]], axis=0)


def layers_kernel(half_ref, lengths_ref, flat_ref, rows_ref, w_in_hbm, w_out_hbm, cot_hbm, *rest):
    out_hbm, sent_hbm, back_hbm, kept_ref = rest[:4]
    w_in_ref, w_out_ref, cot_ref, out_ref, emb_t_ref, gated_t_ref, dpre_ref, grad_ref, sent_ref, back_ref = rest[4:14]
    emb_ref, hidden_ref, slope_ref, weight_ref, dsilu_ref, att_ref, datt_ref, in_sem, out_sem = rest[14:]
    slots = rows_ref.shape[0]
    width = w_out_ref.shape[0]
    length = cot_hbm.shape[1]
    width4 = w_in_ref.shape[1]
    chunk = 512
    chunks = [slice(first, first + chunk) for first in range(0, width4, chunk)]
    incoming = []

    def bring(source, target):
        incoming.append(pltpu.make_async_copy(source, target, in_sem.at[len(incoming)]))
        incoming[-1].start()

    for part in chunks:
        at = pl.ds(part.start, chunk)
        bring(w_in_hbm.at[:, at], w_in_ref.at[:, at])
    bring(w_out_hbm, w_out_ref)
    bring(cot_hbm, cot_ref)
    outgoing = []

    def send(source, target):
        outgoing.append(pltpu.make_async_copy(source, target, out_sem.at[len(outgoing)]))
        outgoing[-1].start()

    of = [slice(micro * length, (micro + 1) * length) for micro in range(MB)]
    for micro in range(MB):
        column = column_of(flat_ref[micro : micro + 1, :])

        def placed(shift, column=column):
            lanes = iota((length, 128), 1).astype(F32)
            parts = [
                jnp.where(column == lanes + float(first - shift), 1.0, 0.0).astype(BF16)
                for first in range(0, slots, 128)
            ]
            return jnp.concatenate(parts, axis=1)

        if micro == 2:
            rows = rows_ref[:, width:]
            embedded = jnp.concatenate([mm(placed(0), rows), mm(placed(4), rows)], axis=1)
        else:
            embedded = mm(placed(4 * micro), rows_ref[:, :width])
        emb_ref[of[micro], :] = embedded.astype(BF16)
        emb_t_ref[:, of[micro]] = jnp.transpose(embedded).astype(BF16)

    for which, at in enumerate(chunks):
        incoming[which].wait()
        half = mm(emb_ref[...], w_in_ref[:, at]) * 0.5
        tanh = jnp.tanh(half)
        act = half + half * tanh
        hidden_ref[:, at] = act.astype(BF16)
        slope_ref[:, at] = (0.5 * ((1.0 + tanh) + act * (1.0 - tanh))).astype(BF16)

    lane = iota((1, 128), 1)
    first_head = (lane < 64).astype(F32)
    second_head = 1.0 - first_head
    masks = (first_head.astype(BF16), second_head.astype(BF16))
    score_masks = ((first_head * 0.0625).astype(BF16), (second_head * 0.0625).astype(BF16))
    pairs = HEADS // 2
    query_at = iota((length, length), 0)
    key_at = iota((length, length), 1)
    for micro in range(MB):
        ends = []
        total = 0
        for which in range(3):
            total = total + lengths_ref[micro, 0, which]
            ends.append(total)

        def segment(places, ends=ends):
            return sum((places >= end).astype(I32) for end in ends)

        allowed = (segment(query_at) == segment(key_at)) & (key_at <= query_at)
        for pair in range(pairs):
            first = 128 * pair
            value = hidden_ref[of[micro], width + first : width + first + 128]
            query = hidden_ref[of[micro], 2 * width + first : 2 * width + first + 128]
            key = hidden_ref[of[micro], 3 * width + first : 3 * width + first + 128]
            halves = mm_nt(both_heads(query, score_masks), key)
            for head in range(2):
                at = slice(length * head, length * head + length)
                half = halves[at]
                tanh = jnp.tanh(half)
                act = half + half * tanh
                weight_ref[micro * pairs + pair, :, at] = jnp.where(allowed, act, 0.0).astype(BF16)
                dsilu_ref[micro * pairs + pair, :, at] = jnp.where(
                    allowed, (1.0 + tanh) + act * (1.0 - tanh), 0.0
                ).astype(BF16)
            att_ref[of[micro], first : first + 128] = mm(
                weight_ref[micro * pairs + pair], both_heads(value, masks)
            )

    incoming[-2].wait()
    incoming[-1].wait()
    cot = cot_ref[...].reshape(MB * length, width)
    dgated_all = mm_nt(cot, w_out_ref[...])
    gated_all = []
    for micro in range(MB):
        attended = att_ref[of[micro], :]
        centred = attended - jnp.mean(attended, axis=1, keepdims=True)
        inverse = lax.rsqrt(jnp.mean(centred * centred, axis=1, keepdims=True) + 1e-05)
        normed = centred * inverse
        gate = hidden_ref[of[micro], :width].astype(F32)
        gated = normed * gate
        gated_t_ref[:, of[micro]] = jnp.transpose(gated).astype(BF16)
        gated_all.append(gated.astype(BF16))
        dgated = dgated_all[of[micro]]
        dgate = dgated * normed
        dnormed = dgated * gate
        dpre_ref[of[micro], :width] = (dgate * slope_ref[of[micro], :width].astype(F32)).astype(BF16)
        shared = jnp.mean(dnormed * normed, axis=1, keepdims=True)
        dcentred = inverse * (dnormed - normed * shared)
        datt = dcentred - jnp.mean(dcentred, axis=1, keepdims=True)
        datt_ref[of[micro], :] = datt.astype(BF16)
    mixed = mm(jnp.concatenate(gated_all, axis=0), w_out_ref[...])
    out_ref[...] = (emb_ref[...].astype(F32) + mixed).astype(BF16).reshape(out_ref.shape)
    send(out_ref, out_hbm)

    for micro in range(MB):
        for pair in range(pairs):
            first = 128 * pair
            at_value = slice(width + first, width + first + 128)
            at_query = slice(2 * width + first, 2 * width + first + 128)
            at_key = slice(3 * width + first, 3 * width + first + 128)
            value = hidden_ref[of[micro], at_value]
            query = hidden_ref[of[micro], at_query]
            key = hidden_ref[of[micro], at_key]
            dhead = datt_ref[of[micro], first : first + 128]
            dweights = mm_nt(both_heads(dhead, masks), value)
            parts = []
            for head in range(2):
                at = slice(length * head, length * head + length)
                parts.append((dweights[at] * dsilu_ref[micro * pairs + pair, :, at].astype(F32)).astype(BF16))
            dscore = jnp.concatenate(parts, axis=1)
            dquery = mm(dscore, both_heads(key, score_masks))
            dkeys = mm_tn(dscore, query * jnp.asarray(0.0625, BF16))
            dkey = jnp.where(lane < 64, dkeys[:length], dkeys[length:])
            dvalues = mm_tn(weight_ref[micro * pairs + pair], dhead)
            dvalue = jnp.where(lane < 64, dvalues[:length], dvalues[length:])
            for at, grad in ((at_value, dvalue), (at_query, dquery), (at_key, dkey)):
                dpre_ref[of[micro], at] = (grad * slope_ref[of[micro], at].astype(F32)).astype(BF16)

    grad_ref[...] = (cot.astype(F32) + mm_nt(dpre_ref[...], w_in_ref[...])).astype(BF16)
    groups, half, columns = sent_ref.shape

    theirs = pl.ds(pl.multiple_of((1 - half_ref[0]) * half, half), half)
    mine = pl.ds(pl.multiple_of(half_ref[0] * half, half), half)

    def split_rows(ref):
        return jnp.concatenate([ref[theirs, :], ref[mine, :]], axis=0)

    def weights(left, right, first):
        part = mm(left, right).astype(BF16)
        start = first
        while start < first + right.shape[1]:
            group, inside = start // columns, start % columns
            count = min(columns - inside, first + right.shape[1] - start)
            here = part[:, start - first : start - first + count]
            sent_ref[group, :, inside : inside + count] = here[:half]
            kept_ref[group * half : (group + 1) * half, inside : inside + count] = here[half:]
            start += count

    left = split_rows(emb_t_ref)
    for first in range(0, width4, 512):
        weights(left, dpre_ref[:, first : first + 512], first)
    weights(split_rows(gated_t_ref), cot, width4)
    send(sent_ref, sent_hbm)
    places = iota((slots, length), 0)

    def placing(micro, shift):
        return jnp.where(places == flat_ref[micro : micro + 1, :] + shift, 1.0, 0.0).astype(BF16)

    pair = jnp.concatenate([placing(0, 0), placing(1, 4)], axis=1)
    back_ref[:, :width] = mm(pair, grad_ref[: 2 * length]).astype(BF16)
    last = jnp.concatenate([placing(2, 0), placing(2, 4)], axis=1)
    halves = [grad_ref[2 * length :, : width // 2], grad_ref[2 * length :, width // 2 :]]
    back_ref[:, width:] = mm(last, jnp.concatenate(halves, axis=0)).astype(BF16)
    send(back_ref, back_hbm)
    for copy in outgoing:
        copy.wait()


def layers(core, lengths, flat, rows, w_in, w_out, cotangent):
    width = w_in.shape[0]
    length = cotangent.shape[1]
    slots = rows.shape[0]
    columns = 5 * width // 4
    sent = (4, width // 2, columns)
    return pl.pallas_call(
        layers_kernel,
        out_shape=[
            jax.ShapeDtypeStruct(shape, BF16) for shape in [cotangent.shape, sent, rows.shape, (slots, columns)]
        ],
        in_specs=[SMEM, SMEM, VMEM, VMEM] + [HBM] * 3,
        out_specs=[HBM, HBM, HBM, VMEM],
        scratch_shapes=[
            pltpu.VMEM(shape, BF16)
            for shape in [
                w_in.shape,
                w_out.shape,
                cotangent.shape,
                cotangent.shape,
                (width, MB * length),
                (width, MB * length),
                (MB * length, 4 * width),
                (MB * length, width),
                sent,
                rows.shape,
                (MB * length, width),
                (MB * length, 4 * width),
                (MB * length, 4 * width),
                (MB * HEADS // 2, length, 2 * length),
                (MB * HEADS // 2, length, 2 * length),
            ]
        ]
        + [
            pltpu.VMEM((MB * length, width), F32),
            pltpu.VMEM((MB * length, width), BF16),
            pltpu.SemaphoreType.DMA((10,)),
            pltpu.SemaphoreType.DMA((3,)),
        ],
        compiler_params=params(46),
        cost_estimate=cost(28_000_000_000, 10 * 1024 * 1024),
        name="layers",
    )(core, lengths, flat, rows, w_in, w_out, cotangent)


def message_kernel(back_hbm, kept_ref, other_ref, out_ref, sem):
    skip = back_hbm.shape[1]
    copy = pltpu.make_async_copy(back_hbm, out_ref.at[:, pl.ds(0, skip)], sem)
    copy.start()
    out_ref[:, skip:] = (kept_ref[...].astype(F32) + other_ref[...].astype(F32)).astype(BF16)
    copy.wait()


def message(back, kept, other):
    return pl.pallas_call(
        message_kernel,
        out_shape=jax.ShapeDtypeStruct((back.shape[0], back.shape[1] + kept.shape[1]), BF16),
        in_specs=[HBM, VMEM, VMEM],
        out_specs=VMEM,
        scratch_shapes=[pltpu.SemaphoreType.DMA],
        compiler_params=params(16),
        cost_estimate=cost(1_000_000, 4 * 1024 * 1024),
        name="message",
    )(back, kept, other)


def shard_sum_kernel(in_ref, out_ref, *, skip, factor):
    slots = in_ref.shape[0]
    parts = in_ref[:, skip:].astype(F32).reshape(slots // 16, 16, in_ref.shape[1] - skip)
    summed = (jnp.sum(parts, axis=0) * factor).astype(BF16)
    out_ref[...] = jnp.broadcast_to(summed[None], (slots // 16, *summed.shape)).reshape(out_ref.shape)


def shard_sum(arrived, skip, factor):
    slots = arrived.shape[0]
    return pl.pallas_call(
        functools.partial(shard_sum_kernel, skip=skip, factor=factor),
        out_shape=jax.ShapeDtypeStruct((slots, arrived.shape[1] - skip), BF16),
        in_specs=[VMEM],
        out_specs=VMEM,
        compiler_params=params(16),
        cost_estimate=cost(1_000_000, 4 * 1024 * 1024),
        name="shard_sum",
    )(arrived)


def table_grad_kernel(pair_row_ref, last_row_ref, arrived_ref, out_ref, last_rows_ref):
    step = pl.program_id(0)
    block, width = out_ref.shape

    @pl.when(step == 0)
    def _():
        last_rows_ref[...] = unfold(arrived_ref[:, width : width + width // 2].astype(F32)).astype(BF16)

    def hot(row):
        places = iota((block, row.shape[1]), 0)
        return jnp.where(places == row - step * block, 1.0, 0.0).astype(BF16)

    out_ref[...] = mm(hot(pair_row_ref[...]), arrived_ref[:, :width]) + mm(
        hot(last_row_ref[...]), last_rows_ref[...]
    )


def table_gradient(pair_row, last_row, arrived, own_rows, width):
    steps = 8
    block = own_rows // steps

    def whole(shape):
        return pl.BlockSpec(shape, lambda i: (0,) * len(shape))

    return pl.pallas_call(
        table_grad_kernel,
        out_shape=jax.ShapeDtypeStruct((own_rows, width), F32),
        grid=(steps,),
        in_specs=[whole(pair_row.shape), whole(last_row.shape), whole(arrived.shape)],
        out_specs=pl.BlockSpec((block, width), lambda i: (i, 0)),
        scratch_shapes=[pltpu.VMEM((last_row.shape[1], width), BF16)],
        compiler_params=params(24),
        cost_estimate=cost(2 * own_rows * 1536 * width, 12 * 1024 * 1024),
        name="table_grad",
    )(pair_row, last_row, arrived)


def finish_kernel(core_ref, in_ref, *rest):
    del core_ref
    win_ref, wout_ref = rest[-2:]
    groups, _, _, columns = in_ref.shape
    width4 = win_ref.shape[-1]
    for group in range(groups):
        first = group * columns
        last = min(first + columns, width4)
        part = in_ref[group].astype(F32)
        for half in range(2):
            rows = part[:, 8 * half : 8 * half + 8]
            win_ref[half, :, 0, :, first:last] = rows[:, :, : last - first]
            if group == groups - 1:
                wout_ref[half, :, 0] = rows[:, :, last - first :]


def finish(core, part, before, width, width4):
    across = width // 32
    part = part.reshape(4, across, 16, part.shape[1])
    steps = 2
    block = across // steps
    shapes = [(2, across, 2, 8, width4), (2, across, 2, 8, width)]
    return pl.pallas_call(
        finish_kernel,
        out_shape=[jax.ShapeDtypeStruct(shape, F32) for shape in shapes],
        grid_spec=pltpu.PrefetchScalarGridSpec(
            num_scalar_prefetch=1,
            grid=(steps,),
            in_specs=[pl.BlockSpec((4, block, 16, part.shape[3]), lambda i, which: (0, i, 0, 0))]
            + [pl.BlockSpec(memory_space=pl.ANY)] * len(before),
            out_specs=[
                pl.BlockSpec((2, block, 1, 8, shape[4]), lambda i, which: (0, i, which[0], 0, 0)) for shape in shapes
            ],
        ),
        input_output_aliases={2: 0, 3: 1} if before else {},
        compiler_params=params(16),
        cost_estimate=cost(1_000_000, 4 * 1024 * 1024),
        name=f"finish{len(before)}",
    )(core, part, *before)


def trade(payload, axes=AXES):
    return lax.all_to_all(payload, axes, split_axis=0, concat_axis=0, tiled=True)


def shards(table, w_in, w_out, item_owner, item_slot, seq_lengths, cotangent):
    owners_n = lax.axis_size(AXES)
    length = item_slot.shape[1]
    own_rows, width = table.shape
    slots = owners_n * 8
    core = lax.axis_index("core").astype(I32).reshape(1)
    swap = [(0, 1), (1, 0)]

    wanted, flat = requests(item_owner.reshape(MB, 1, length), item_slot, owners_n)
    asked = trade(wanted)
    rows = trade(gather(asked, table))
    pair_row = asked[:, :8].reshape(1, slots)
    last_row = asked[:, 8:12].reshape(1, slots // 2)
    out, sent, back, kept = layers(core, seq_lengths, flat, rows, w_in, w_out, cotangent)
    columns = sent.shape[2]
    other = lax.ppermute(sent.reshape(slots, columns), "core", swap)
    arrived = trade(message(back, kept, other))
    factor = (MB * length * owners_n) ** (-0.5)
    mine_full = trade(shard_sum(arrived, rows.shape[1], factor), AXES[:2])
    table_grad = table_gradient(pair_row, last_row, arrived, own_rows, width)
    mine_full, table_grad = lax.optimization_barrier((mine_full, table_grad))
    other_full = lax.ppermute(mine_full, "core", swap)
    width4 = w_in.shape[1]
    partial = finish(core, mine_full, (), width, width4)
    win_grad, wout_grad = finish(1 - core, other_full, partial, width, width4)
    return out, table_grad, win_grad.reshape(width, width4), wout_grad.reshape(width, width)


def solution(mesh):
    dp, table_axis = mesh.devices.shape
    mesh = Mesh(mesh.devices.reshape(dp, table_axis // 2, 2), AXES)
    in_specs = (
        P(AXES, None),
        P(),
        P(),
        P(None, AXES, None),
        P(None, AXES),
        P(None, AXES, None),
        P(None, AXES, None),
    )
    out_specs = (P(None, AXES, None), P(AXES, None), P(), P())
    return jax.shard_map(shards, mesh=mesh, in_specs=in_specs, out_specs=out_specs, check_vma=False)
```
